256 devices in a mesh: frame: 32 (over z_lo, x, core), fsdp: 8 (over y, z_hi).
Axes of the slice: x: 4, y: 4, z: 8 (z_hi: 2, z_lo: 4; z = z_hi * 4 + z_lo), core: 2. Of those that a mesh axis runs over, the one named last changes fastest.
Arguments:
- tokens: bfloat16 [32, 16, 32, 3072], P('frame', 'fsdp'), may hold values from -48 to 48
- frame_time: int32 [32], replicated, may hold values from 0 to 15
- qkv_weight: bfloat16 [3, 3072, 2048], P(None, 'frame', 'fsdp'), may hold values from -0.109375 to 0.109375
- out_weight: bfloat16 [2048, 3072], P('fsdp', 'frame'), may hold values from -2 to 2
- norm_gain: bfloat16 [3072], replicated, may hold values from 0.099609375 to 1.8984375
- conv_weight: bfloat16 [3, 3, 3072], replicated, may hold values from -2 to 2
- up_weight: bfloat16 [3072, 3072], P('frame', 'fsdp'), may hold values from -0.109375 to 0.109375
- down_weight: bfloat16 [3072, 3072], P('fsdp', 'frame'), may hold values from -0.109375 to 0.109375
Outputs:
- layer_out: bfloat16 [32, 16, 32, 3072], P('frame', 'fsdp')
The draws below stay inside these ranges and needn't reach their ends.
All inputs are finite; a program needn't handle non-finite values.
Results may differ from the reference program's by a relative error of at most 0.019.
The reference program's roundings to bfloat16 on the way (of `weights`, `attention`, `normed`, `conved` and `hidden`) count: a program that leaves them out, or rounds other values in their place, can miss the bound.
Values may be sent and summed in bfloat16 or wider, within the bound.
A program may use at most 192 MiB of HBM per device.

```python
import math
import jax
import jax.numpy as jnp
from jax import lax

D = 3072
HEADS = 16
HEAD = 128
FF = 3072
COLS = 32
FRAMES = 32
FRAME_ROWS = 16
TOK_FRAME = 512


def draw_tokens(key, part):
    base = jax.random.normal(key, (FRAMES, FRAME_ROWS, COLS, D), jnp.float32)
    base = jnp.clip(base, -6.0, 6.0)
    return base.astype(jnp.bfloat16)


def with_ends(array, own_key, low, largest):
    longest = array.shape.index(max(array.shape))
    spots = []
    for shift in (0, 1):
        where = [jax.random.randint(jax.random.fold_in(own_key, axis), (), 0, length) for axis, length in enumerate(array.shape)]
        where[longest] = (where[longest] + shift) % array.shape[longest]
        spots.append(tuple(where))
    return array.at[spots[0]].set(low).at[spots[1]].set(largest)


def level_of(rng, extent, split, least, largest):
    def one(axis_at, blocks):
        steps = jax.random.uniform(jax.random.fold_in(jax.random.fold_in(rng, 6), axis_at), (blocks,), jnp.float32, least / len(split), largest / len(split))
        return jnp.repeat(jnp.exp(steps), extent[axis_at] // blocks).reshape((-1,) + (1,) * (len(extent) - axis_at - 1))

    level = one(*split[0])
    for cut in split[1:]:
        level = level * one(*cut)
    return level


def noise(own_key, shape, deviation, limit, cuts=(), kind=jnp.bfloat16):
    array = jax.random.normal(own_key, shape, jnp.float32) * deviation
    if len(cuts) > 0:
        array = level_of(own_key, shape, cuts, -0.22, 0.18) * array
    return jnp.clip(array, min=-limit, max=limit).astype(kind)


def setup_inputs(seed: int = 0) -> dict:
    key_of = jax.random.split(jax.random.key(seed), 9)
    tokens = draw_tokens(jax.random.fold_in(key_of[8], 71), 0)
    frame_time = with_ends(jax.random.randint(key_of[1], (FRAMES,), 0, FRAMES // 2), jax.random.fold_in(key_of[1], 1), 0, (FRAMES // 2) - 1).astype(jnp.int32)
    qkv_weight = noise(key_of[2], (3, D, HEADS * HEAD), D ** -0.5, 0.109375, ((1, 32), (2, 8)))
    out_weight = noise(key_of[3], (HEADS * HEAD, D), (max(HEADS * HEAD // 256, 1)) ** -0.5, 2.0, ((0, 8), (1, 32)))
    norm_gain = jnp.clip(1.0 + 0.18 * jax.random.normal(key_of[4], (D,), jnp.float32), 0.099609375, 1.8984375).astype(jnp.bfloat16)
    conv_weight = noise(key_of[5], (3, 3, D), 9 ** -0.5, 2.0)
    up_weight = noise(key_of[6], (D, FF), D ** -0.5, 0.109375, ((0, 32), (1, 8)))
    down_weight = noise(key_of[7], (FF, D), FF ** -0.5, 0.109375, ((0, 8), (1, 32)))
    return dict(tokens=tokens, frame_time=frame_time, qkv_weight=qkv_weight, out_weight=out_weight, norm_gain=norm_gain, conv_weight=conv_weight, up_weight=up_weight, down_weight=down_weight)


def reference(tokens, frame_time, qkv_weight, out_weight, norm_gain, conv_weight, up_weight, down_weight):
    inner = HEADS * HEAD
    flat = tokens.reshape(FRAMES * TOK_FRAME, D)
    queries = lax.optimization_barrier(jnp.dot(flat, qkv_weight[0], preferred_element_type=jnp.float32).astype(jnp.bfloat16))
    keys = lax.optimization_barrier(jnp.dot(flat, qkv_weight[1], preferred_element_type=jnp.float32).astype(jnp.bfloat16))
    values = lax.optimization_barrier(jnp.dot(flat, qkv_weight[2], preferred_element_type=jnp.float32).astype(jnp.bfloat16))
    keys_wide = keys.astype(jnp.float32).reshape(FRAMES * TOK_FRAME, HEADS, HEAD)
    values_wide = values.astype(jnp.float32).reshape(FRAMES * TOK_FRAME, HEADS, HEAD)
    key_time = jnp.repeat(frame_time, TOK_FRAME)
    factor = 1.0 / math.sqrt(HEAD)

    def attend(index):
        block = lax.dynamic_slice_in_dim(queries, (index * TOK_FRAME).astype(jnp.int32), TOK_FRAME, 0)
        block = block.astype(jnp.float32).reshape(TOK_FRAME, HEADS, HEAD)
        own_time = frame_time[index]
        scores = jnp.einsum('qhd,khd->hqk', block, keys_wide) * factor
        scores = jnp.where((key_time <= own_time)[None, None, :], scores, -jnp.inf)
        highest = lax.optimization_barrier(jnp.max(scores, axis=-1, keepdims=True))
        weights = jnp.exp(scores - highest)
        summed = lax.optimization_barrier(jnp.sum(weights, axis=-1))
        rounded = lax.optimization_barrier(weights.astype(jnp.bfloat16)).astype(jnp.float32)
        mixed = jnp.einsum('hqk,khd->qhd', rounded, values_wide)
        return (mixed / summed.T[:, :, None]).reshape(TOK_FRAME, inner).astype(jnp.bfloat16)
    attention = lax.map(attend, jnp.arange(FRAMES, dtype=jnp.int32)).reshape(FRAMES * TOK_FRAME, inner)
    projected = jnp.dot(attention, out_weight, preferred_element_type=jnp.float32)
    residual = tokens.astype(jnp.float32) + projected.reshape(FRAMES, FRAME_ROWS, COLS, D)
    mean_square = lax.optimization_barrier(jnp.mean(residual * residual, axis=-1, keepdims=True))
    normed = (residual * lax.rsqrt(mean_square + 1e-06) * norm_gain.astype(jnp.float32)).astype(jnp.bfloat16)
    normed = lax.optimization_barrier(normed)
    padded = jnp.pad(normed, ((0, 0), (1, 1), (1, 1), (0, 0)))
    kernel = conv_weight.astype(jnp.float32)
    conved = jnp.zeros((FRAMES, FRAME_ROWS, COLS, D), jnp.float32)
    for vertical in range(3):
        for lateral in range(3):
            window = padded[:, vertical:vertical + FRAME_ROWS, lateral:lateral + COLS, :].astype(jnp.float32)
            conved = conved + window * kernel[vertical, lateral]
    conved = conved.astype(jnp.bfloat16).reshape(FRAMES * TOK_FRAME, D)
    hidden = jax.nn.gelu(jnp.dot(conved, up_weight, preferred_element_type=jnp.float32)).astype(jnp.bfloat16)
    lowered = jnp.dot(hidden, down_weight, preferred_element_type=jnp.float32)
    return (residual + lowered.reshape(FRAMES, FRAME_ROWS, COLS, D)).astype(jnp.bfloat16)
```

```python
import functools
import math

import jax
import jax.numpy as jnp
from jax import lax
from jax.experimental import pallas as pl
from jax.experimental.pallas import tpu as pltpu
from jax.sharding import Mesh
from jax.sharding import PartitionSpec as P

HEAD = 128
MESH = pl.DeviceIdType.MESH
BF = jnp.bfloat16
F32 = jnp.float32
AXES = ("zlo", "x", "core", "y", "zhi")
ANY = pl.BlockSpec(memory_space=pl.ANY)
VMEM = pl.BlockSpec(memory_space=pltpu.VMEM)
SMEM = pl.BlockSpec(memory_space=pltpu.SMEM)
SCALE2 = math.log2(math.e) / math.sqrt(HEAD)


def aligned(index, size):
    return pl.ds(pl.multiple_of(index * size, size), size)


class Place:
    def __init__(self):
        self.zlo, self.x, self.core, self.y, self.zhi = (lax.axis_index(a) for a in AXES)
        turn = 1 - 2 * self.core
        self.chip = self.zlo * 4 + self.x
        self.share = 2 * self.y + self.zhi
        self.xf, self.xb, self.xo = (lax.rem(self.x + 4 + k, 4) for k in (turn, -turn, 2))
        self.yf, self.yb, self.yo = (lax.rem(self.y + 4 + k, 4) for k in (turn, -turn, 2))
        self.partner = {"core": 1 - self.core}
        self.far = {"zhi": 1 - self.zhi}


class Copies:
    def __init__(self, send, recv, local):
        self.send, self.recv, self.local = send, recv, local
        self.pushed, self.kept, self.count = [], [], 0

    def push(self, src, dst, device):
        index = self.count
        self.count += 1
        copy = pltpu.make_async_remote_copy(
            src, dst, self.send.at[index], self.recv.at[index], device_id=device, device_id_type=MESH
        )
        copy.start()
        self.pushed.append(copy)
        return index

    def got(self, index, region):
        pltpu.make_async_copy(region, region, self.recv.at[index]).wait()

    def keep(self, src, dst):
        copy = pltpu.make_async_copy(src, dst, self.local.at[len(self.kept)])
        copy.start()
        self.kept.append(copy)
        return copy

    def sent(self):
        for copy in self.pushed:
            copy.wait_send()


def greet(devices):
    barrier = pltpu.get_barrier_semaphore()
    for device in devices:
        pl.semaphore_signal(barrier, inc=1, device_id=device, device_id_type=MESH)
    pl.semaphore_wait(barrier, len(devices))


def x_start(copies, at, region, z):
    mine = region(z * 4 + at.x)
    return (
        copies.push(mine, mine, {"x": at.xf}),
        copies.push(mine, mine, {"x": at.xb}),
    )


def x_forward(copies, at, region, z, started):
    block = region(z * 4 + at.xb)
    copies.got(started[0], block)
    return copies.push(block, block, {"x": at.xf})


def x_rest(copies, at, region, z, started, forwarded):
    copies.got(started[1], region(z * 4 + at.xf))
    copies.got(forwarded, region(z * 4 + at.xo))


def scratch(pushes, locals_):
    return [
        pltpu.SemaphoreType.DMA((pushes,)),
        pltpu.SemaphoreType.DMA((pushes,)),
        pltpu.SemaphoreType.DMA((locals_,)),
    ]


def spread_kernel(tok, wq, wo, tok_all, wq_all, wo_all, send, recv, local):
    at = Place()
    copies = Copies(send, recv, local)
    zs = [lax.rem(at.zlo + k, 4) for k in (1, 3, 2)]
    zfrom = [lax.rem(at.zlo + 4 - k, 4) for k in (1, 3, 2)]
    greet(
        [at.partner, at.far, {"y": at.yf}, {"y": at.yb}, {"x": at.xf}, {"x": at.xb}]
        + [{"zlo": z} for z in zs]
    )

    def piece(share, half):
        return tok_all.at[at.core, share, pl.ds(32 * half, 32)]

    def wq_block(chip):
        return wq_all.at[:, aligned(chip, 192)]

    def wo_block(chip):
        return wo_all.at[:, chip]

    halves = (0, 1)
    source = [tok.at[pl.ds(32 * h, 32)] for h in halves]
    rows = wq_all.at[:, aligned(2 * at.chip + at.core, 96)]
    w_pair = copies.push(wq.at[:, :, aligned(1 - at.core, HEAD)], rows, at.partner)
    w_own = copies.keep(wq.at[:, :, aligned(at.core, HEAD)], rows)
    o_far = copies.push(wo, wo_all.at[at.zhi, at.chip], at.far)
    o_own = copies.keep(wo, wo_all.at[at.zhi, at.chip])
    far = [copies.push(source[h], piece(at.share, h), at.far) for h in halves]
    own_f = [copies.push(source[h], piece(at.share, h), {"y": at.yf}) for h in halves]
    own_b = [copies.push(source[h], piece(at.share, h), {"y": at.yb}) for h in halves]
    t_own = copies.keep(tok, tok_all.at[at.core, at.share])

    partner_rows = wq_all.at[:, aligned(2 * at.chip + 1 - at.core, 96)]
    copies.got(w_pair, partner_rows)
    w_own.wait()
    w_z = [copies.push(wq_block(at.chip), wq_block(at.chip), {"zlo": z}) for z in zs]
    w_x = [x_start(copies, at, wq_block, at.zlo)]
    copies.got(o_far, wo_all.at[1 - at.zhi, at.chip])
    o_own.wait()
    o_z = [copies.push(wo_block(at.chip), wo_block(at.chip), {"zlo": z}) for z in zs]
    o_x = [x_start(copies, at, wo_block, at.zlo)]

    shared = []

    def share_out(share):
        block = tok_all.at[at.core, share]
        shared.append((copies.push(block, block, at.partner), share))

    t_own.wait()
    share_out(at.share)
    back = 2 * at.yb + at.zhi
    ahead = 2 * at.yf + at.zhi
    beyond = 2 * at.yo + at.zhi
    fwd = []
    for h in halves:
        copies.got(own_f[h], piece(back, h))
        fwd.append(copies.push(piece(back, h), piece(back, h), {"y": at.yf}))
    w_f = [x_forward(copies, at, wq_block, at.zlo, w_x[0])]
    o_f = [x_forward(copies, at, wo_block, at.zlo, o_x[0])]
    share_out(back)
    for h in halves:
        copies.got(own_b[h], piece(ahead, h))
    share_out(ahead)
    far_share = 2 * at.y + 1 - at.zhi
    far_f, far_b = [], []
    for h in halves:
        copies.got(far[h], piece(far_share, h))
        far_f.append(copies.push(piece(far_share, h), piece(far_share, h), {"y": at.yf}))
        far_b.append(copies.push(piece(far_share, h), piece(far_share, h), {"y": at.yb}))
    share_out(far_share)
    for k in range(3):
        copies.got(w_z[k], wq_block(zfrom[k] * 4 + at.x))
        w_x.append(x_start(copies, at, wq_block, zfrom[k]))
        copies.got(o_z[k], wo_block(zfrom[k] * 4 + at.x))
        o_x.append(x_start(copies, at, wo_block, zfrom[k]))
    for h in halves:
        copies.got(fwd[h], piece(beyond, h))
    share_out(beyond)
    back, ahead, beyond = back + 1 - 2 * at.zhi, ahead + 1 - 2 * at.zhi, beyond + 1 - 2 * at.zhi
    w_f.append(x_forward(copies, at, wq_block, zfrom[0], w_x[1]))
    o_f.append(x_forward(copies, at, wo_block, zfrom[0], o_x[1]))
    fwd = []
    for h in halves:
        copies.got(far_f[h], piece(back, h))
        fwd.append(copies.push(piece(back, h), piece(back, h), {"y": at.yf}))
    share_out(back)
    for k in (1, 2):
        w_f.append(x_forward(copies, at, wq_block, zfrom[k], w_x[k + 1]))
        o_f.append(x_forward(copies, at, wo_block, zfrom[k], o_x[k + 1]))
    for h in halves:
        copies.got(far_b[h], piece(ahead, h))
    share_out(ahead)
    for h in halves:
        copies.got(fwd[h], piece(beyond, h))
    share_out(beyond)
    for k, z in enumerate([at.zlo] + zfrom):
        x_rest(copies, at, wq_block, z, w_x[k], w_f[k])
        x_rest(copies, at, wo_block, z, o_x[k], o_f[k])
    for index, share in shared:
        copies.got(index, tok_all.at[1 - at.core, share])
    copies.sent()


def attend_kernel(times, qkv, wo, out, wo_all, kv, top, total, mixed, send, recv, local):
    at = Place()
    copies = Copies(send, recv, local)
    zs = [lax.rem(at.zlo + k, 4) for k in (1, 3, 2)]
    zfrom = [lax.rem(at.zlo + 4 - k, 4) for k in (1, 3, 2)]
    greet(
        [at.partner, {"y": at.yf}, {"y": at.yb}, {"x": at.xf}, {"x": at.xb}]
        + [{"zlo": z} for z in zs]
    )

    def kv_block(chip):
        return kv.at[chip]

    def wo_block(y, core):
        return wo_all.at[pl.ds(2 * y, 2), :, core]

    def attend(chip):
        def tile(t, carry):
            rows = aligned(t, 256)
            own_time = times[2 * at.chip + t // 2]
            scores = lax.dot_general(
                qkv[0, rows, :], kv[chip, 0], (((1,), (1,)), ((), ())), preferred_element_type=F32
            )
            seen = [times[2 * chip + j] <= own_time for j in (0, 1)]
            parts = [scores[:, :512], scores[:, 512:]]
            old = top[rows, :1]
            new = old
            for part, see in zip(parts, seen):
                new = jnp.maximum(
                    new, jnp.where(see, jnp.max(part, axis=1, keepdims=True), -1e30)
                )
            decay = jnp.exp2((old - new) * SCALE2)
            weights = [
                jnp.exp2((part - jnp.where(see, new, 1e30)) * SCALE2)
                for part, see in zip(parts, seen)
            ]
            lanes = total[rows, :] * decay
            for part in weights:
                for j in range(4):
                    lanes = lanes + part[:, 128 * j : 128 * j + 128]
            total[rows, :] = lanes
            top[rows, :] = jnp.broadcast_to(new, (256, 128))
            both = jnp.concatenate([part.astype(BF) for part in weights], axis=1)
            mixed[rows, :] = mixed[rows, :] * decay + jnp.dot(
                both, kv[chip, 1], preferred_element_type=F32
            )
            return carry

        lax.fori_loop(0, 4, tile, 0)

    own = qkv.at[pl.ds(1, 2)]
    kv_z = [copies.push(own, kv_block(at.chip), {"zlo": zs[0]})]
    kv_x = [
        (
            copies.push(own, kv_block(at.chip), {"x": at.xf}),
            copies.push(own, kv_block(at.chip), {"x": at.xb}),
        )
    ]
    first_z = copies.pushed[0]
    kv_own = copies.keep(own, kv_block(at.chip))
    wo_f = copies.push(wo, wo_block(at.y, at.core), {"y": at.yf})
    wo_b = copies.push(wo, wo_block(at.y, at.core), {"y": at.yb})
    wo_own = copies.keep(wo, wo_block(at.y, at.core))
    wo_p = [copies.push(wo, wo_block(at.y, at.core), at.partner)]
    top[...] = jnp.full_like(top, -1e30)
    total[...] = jnp.zeros_like(total)
    mixed[...] = jnp.zeros_like(mixed)
    kv_own.wait()
    attend(at.chip)
    z_sends = [first_z]
    order = [at.zlo] + zfrom
    wo_fwd = None
    for k in range(4):
        z = order[k]
        if k > 0:
            attend(z * 4 + at.x)
        forwarded = x_forward(copies, at, kv_block, z, kv_x[k])
        if k == 0:
            copies.pushed[0].wait_send()
            copies.pushed.pop(0)
            kv_z.append(copies.push(own, kv_block(at.chip), {"zlo": zs[1]}))
            second = copies.pushed.pop()
        if k < 3:
            copies.got(kv_z[k], kv_block(zfrom[k] * 4 + at.x))
            kv_x.append(x_start(copies, at, kv_block, zfrom[k]))
        if k == 0:
            second.wait_send()
            kv_z.append(copies.push(own, kv_block(at.chip), {"zlo": zs[2]}))
        attend(z * 4 + at.xb)
        copies.got(kv_x[k][1], kv_block(z * 4 + at.xf))
        attend(z * 4 + at.xf)
        if k == 1:
            block = wo_block(at.yb, at.core)
            copies.got(wo_f, block)
            wo_fwd = copies.push(block, block, {"y": at.yf})
            wo_p.append(copies.push(block, block, at.partner))
        if k == 2:
            block = wo_block(at.yf, at.core)
            copies.got(wo_b, block)
            wo_p.append(copies.push(block, block, at.partner))
        copies.got(forwarded, kv_block(z * 4 + at.xo))
        attend(z * 4 + at.xo)
    out[...] = (mixed[...] / jnp.sum(total[...], axis=1, keepdims=True)).astype(BF)
    block = wo_block(at.yo, at.core)
    copies.got(wo_fwd, block)
    wo_p.append(copies.push(block, block, at.partner))
    wo_own.wait()
    for index, y in zip(wo_p, (at.y, at.yb, at.yf, at.yo)):
        copies.got(index, wo_block(y, 1 - at.core))
    copies.sent()


def rows_kernel(attn, up, down, rows, ud_all, send, recv, local):
    at = Place()
    copies = Copies(send, recv, local)
    deep = at.zhi * 4 + at.zlo
    z_steps = (1, 7, 2, 6, 3, 5, 4)
    zs = [lax.rem(deep + k, 8) for k in z_steps]
    zfrom = [lax.rem(deep + 8 - k, 8) for k in z_steps]
    peers = [(c, z, y) for y in range(4) for z in (1, 0) for c in (0, 1) if (c, z, y) != (0, 0, 0)]

    def peer(c, z, y, sign):
        return (
            lax.rem(at.core + c, 2),
            lax.rem(at.zhi + z, 2),
            lax.rem(at.y + 4 + sign * y, 4),
        )

    def named(place):
        return {"core": place[0], "zhi": place[1], "y": place[2]}

    greet(
        [named(peer(*p, 1)) for p in peers]
        + [{"x": at.xf}, {"x": at.xb}]
        + [{"zhi": z // 4, "zlo": lax.rem(z, 4)} for z in zs[:-1]]
    )

    def head_rows(head):
        return rows.at[:, aligned(head, HEAD)]

    def needed(place):
        core, zhi, y = place
        first = jnp.clip(2 * (2 * y + zhi) - 1, 0, 12)
        return attn.at[core, pl.ds(pl.multiple_of(first * 32, 32), 128)]

    def ud_block(deep_, x):
        return ud_all.at[:, deep_ // 4, lax.rem(deep_, 4) * 4 + x, at.core]

    def ud_lump(deep_, core):
        return ud_all.at[:, deep_ // 4, aligned(lax.rem(deep_, 4), 4), core]

    head = 2 * at.share + at.core
    mine = (at.core, at.zhi, at.y)
    pushes = [copies.push(needed(peer(*p, 1)), head_rows(head), named(peer(*p, 1))) for p in peers]
    kept = copies.keep(needed(mine), head_rows(head))
    both = [
        copies.keep(up, ud_all.at[0, at.zhi, at.chip, at.core]),
        copies.keep(down, ud_all.at[1, at.zhi, at.chip, at.core]),
    ]
    for copy in both:
        copy.wait()
    own = ud_block(deep, at.x)
    ud_z = [copies.push(own, own, {"zhi": z // 4, "zlo": lax.rem(z, 4)}) for z in zs]

    def start(deep_):
        block = ud_block(deep_, at.x)
        return (copies.push(block, block, {"x": at.xf}), copies.push(block, block, {"x": at.xb}))

    started = [start(deep)]
    order = [deep] + zfrom
    lumps = []
    for k in range(8):
        if k < 7:
            copies.got(ud_z[k], ud_block(zfrom[k], at.x))
            started.append(start(zfrom[k]))
        block = ud_block(order[k], at.xb)
        copies.got(started[k][0], block)
        fwd = copies.push(block, block, {"x": at.xf})
        if k > 0:
            finish(k - 1, before)
        before = fwd

        def finish(j, forwarded):
            copies.got(started[j][1], ud_block(order[j], at.xf))
            copies.got(forwarded, ud_block(order[j], at.xo))
            lump = ud_lump(order[j], at.core)
            lumps.append(copies.push(lump, lump, at.partner))

    finish(7, before)
    kept.wait()
    for index, p in zip(pushes, peers):
        core, zhi, y = peer(*p, -1)
        copies.got(index, head_rows(2 * (2 * y + zhi) + core))
    for index, z in zip(lumps, order):
        copies.got(index, ud_lump(z, 1 - at.core))
    copies.sent()


def project_kernel(rows, wo, out):
    acc = jnp.zeros(out.shape, F32)
    for s in range(8):
        acc = acc + lax.dot_general(
            rows[:, 256 * s : 256 * s + 256],
            wo[s],
            (((1,), (1,)), ((), ())),
            preferred_element_type=F32,
        )
    out[...] = acc


def ring_kernel(part, whole, send, recv, local):
    at = Place()
    copies = Copies(send, recv, local)
    greet([{"y": at.yf}, {"y": at.yb}])
    halves = (0, 1)

    def piece(y, h):
        return whole.at[y, pl.ds(32 * h, 32)]

    source = [part.at[pl.ds(32 * h, 32)] for h in halves]
    ahead = [copies.push(source[h], piece(at.y, h), {"y": at.yf}) for h in halves]
    behind = [copies.push(source[h], piece(at.y, h), {"y": at.yb}) for h in halves]
    own = copies.keep(part, whole.at[at.y])
    fwd = []
    for h in halves:
        copies.got(ahead[h], piece(at.yb, h))
        fwd.append(copies.push(piece(at.yb, h), piece(at.yb, h), {"y": at.yf}))
    for h in halves:
        copies.got(behind[h], piece(at.yf, h))
        copies.got(fwd[h], piece(at.yo, h))
    own.wait()
    copies.sent()


def sum_kernel(terms, out, relay, direct, summed, final, send, recv):
    at = Place()
    copies = Copies(send, recv, None)
    greet([{"y": at.yf}, {"y": at.yb}])
    halves = (0, 1)

    def term(y, h):
        return terms.at[y, pl.ds(32 * h, 32)]

    def half(ref, h):
        return ref.at[pl.ds(32 * h, 32)]

    relays = [copies.push(term(at.yo, h), half(relay, h), {"y": at.yf}) for h in halves]
    directs = [copies.push(term(at.yb, h), half(direct, h), {"y": at.yb}) for h in halves]
    finals = []
    for h in halves:
        copies.got(relays[h], half(relay, h))
        rows = pl.ds(32 * h, 32)
        summed[rows, :] = (terms[at.yf, rows, :].astype(F32) + relay[rows, :].astype(F32)).astype(
            BF
        )
        finals.append(copies.push(half(summed, h), half(final, h), {"y": at.yf}))
    for h in halves:
        rows = pl.ds(32 * h, 32)
        copies.got(directs[h], half(direct, h))
        partial = terms[at.y, rows, :].astype(F32) + direct[rows, :].astype(F32)
        copies.got(finals[h], half(final, h))
        out[rows, :] = partial + final[rows, :].astype(F32)
    copies.sent()


def remote(collective_id, megabytes=32):
    return pltpu.CompilerParams(
        collective_id=collective_id, has_side_effects=True, vmem_limit_bytes=megabytes << 20
    )


def shape(*dims, dtype=BF):
    return jax.ShapeDtypeStruct(dims, dtype)


def grid_conv(window, conv_weight):
    padded = jnp.pad(window, ((0, 0), (1, 1), (0, 0)))
    kernel = conv_weight.astype(F32)
    result = jnp.zeros((2, 32, window.shape[2]), F32)
    for vertical in range(3):
        for lateral in range(3):
            part = padded[vertical : vertical + 2, lateral : lateral + 32, :].astype(F32)
            result = result + part * kernel[vertical, lateral]
    return result.astype(BF)


def shards(
    tokens, frame_time, qkv_weight, out_weight, norm_gain, conv_weight, up_weight, down_weight
):
    width = tokens.shape[3]
    core, y, zhi = (lax.axis_index(a) for a in ("core", "y", "zhi"))
    share = 2 * y + zhi
    tok_all, wq_all, wo_part = pl.pallas_call(
        spread_kernel,
        out_shape=(shape(2, 8, 64, width), shape(3, width, HEAD), shape(2, 16, 96, 256)),
        in_specs=[ANY] * 3,
        out_specs=(ANY,) * 3,
        scratch_shapes=scratch(64, 4),
        compiler_params=remote(1),
    )(tokens.reshape(64, width), qkv_weight, out_weight.T)
    qkv = jnp.einsum(
        "td,idh->ith", tok_all.reshape(1024, width), wq_all, preferred_element_type=F32
    ).astype(BF)
    attn, wo_all = pl.pallas_call(
        attend_kernel,
        out_shape=(shape(1024, HEAD), shape(8, 16, 2, 96, 256)),
        in_specs=[SMEM, VMEM, ANY],
        out_specs=(VMEM, ANY),
        scratch_shapes=[
            pltpu.VMEM((16, 2, 1024, HEAD), BF),
            pltpu.VMEM((1024, HEAD), F32),
            pltpu.VMEM((1024, HEAD), F32),
            pltpu.VMEM((1024, HEAD), F32),
        ]
        + scratch(24, 2),
        compiler_params=remote(2, 40),
    )(frame_time, qkv, wo_part)
    rows, ud_all = pl.pallas_call(
        rows_kernel,
        out_shape=(shape(128, 16 * HEAD), shape(2, 2, 16, 2, 96, 384)),
        in_specs=[ANY] * 3,
        out_specs=(ANY,) * 2,
        scratch_shapes=scratch(64, 3),
        compiler_params=remote(3),
    )(attn.reshape(2, 512, HEAD), up_weight, down_weight.T)
    projected = pl.pallas_call(
        project_kernel,
        grid=(12,),
        out_shape=shape(128, width, dtype=F32),
        in_specs=[
            pl.BlockSpec((128, 16 * HEAD), lambda n: (0, 0)),
            pl.BlockSpec((8, 256, 256), lambda n: (0, n, 0)),
        ],
        out_specs=pl.BlockSpec((128, 256), lambda n: (0, n)),
    )(rows, wo_all.reshape(8, width, 256))
    first = jnp.clip(2 * share - 1, 0, 12)
    frame = lax.dynamic_index_in_dim(tok_all, core, 0, keepdims=False).reshape(16, 32, width)
    near = lax.dynamic_slice_in_dim(frame, first, 4, 0)
    residual = near.astype(F32) + projected.reshape(4, 32, width)
    mean_square = jnp.mean(residual * residual, axis=-1, keepdims=True)
    normed = (residual * lax.rsqrt(mean_square + 1e-06) * norm_gain.astype(F32)).astype(BF)
    shift = 2 * share - 1 - first
    window = lax.dynamic_slice_in_dim(
        jnp.pad(normed, ((1, 1), (0, 0), (0, 0))), 1 + shift, 4, 0
    )
    own_residual = lax.dynamic_slice_in_dim(residual, 1 + shift, 2, 0)
    conved = grid_conv(window, conv_weight).reshape(64, width)
    gathered = pl.pallas_call(
        ring_kernel,
        out_shape=shape(4, 64, width),
        in_specs=[ANY],
        out_specs=ANY,
        scratch_shapes=scratch(8, 1),
        compiler_params=remote(4),
    )(conved).reshape(256, width)
    up_all = ud_all[0].reshape(2, width, 384)
    down_all = ud_all[1].reshape(2, width, 384)
    lowered = jnp.zeros((256, width), F32)
    for z in range(2):
        hidden = jax.nn.gelu(jnp.dot(gathered, up_all[z], preferred_element_type=F32)).astype(BF)
        lowered = lowered + lax.dot_general(
            hidden, down_all[z], (((1,), (1,)), ((), ())), preferred_element_type=F32
        )
    summed = pl.pallas_call(
        sum_kernel,
        out_shape=shape(64, width, dtype=F32),
        in_specs=[VMEM],
        out_specs=VMEM,
        scratch_shapes=[pltpu.VMEM((64, width), BF)] * 4 + scratch(8, 1)[:2],
        compiler_params=remote(5),
    )(lowered.astype(BF).reshape(4, 64, width))
    return (own_residual + summed.reshape(2, 32, width)).astype(BF)[None]


def solution(mesh):
    fine = Mesh(mesh.devices.reshape(4, 4, 2, 4, 2), AXES)
    frame, fsdp = ("zlo", "x", "core"), ("y", "zhi")
    placed = (
        P(frame, fsdp, None, None),
        P(),
        P(None, frame, fsdp),
        P(fsdp, frame),
        P(),
        P(),
        P(frame, fsdp),
        P(fsdp, frame),
    )
    return jax.shard_map(
        shards,
        mesh=fine,
        in_specs=placed,
        out_specs=P(frame, fsdp, None, None),
        check_vma=False,
    )
```

```python
import math

import jax
import jax.numpy as jnp
from jax import lax
from jax.experimental import pallas as pl
from jax.experimental.pallas import tpu as pltpu
from jax.sharding import Mesh
from jax.sharding import PartitionSpec as P

HEAD = 128
MESH = pl.DeviceIdType.MESH
BF = jnp.bfloat16
F32 = jnp.float32
AXES = ("zlo", "x", "core", "y", "zhi")
ANY = pl.BlockSpec(memory_space=pl.ANY)
VMEM = pl.BlockSpec(memory_space=pltpu.VMEM)
SMEM = pl.BlockSpec(memory_space=pltpu.SMEM)
SCALE2 = math.log2(math.e) / math.sqrt(HEAD)


def aligned(index, size):
    return pl.ds(pl.multiple_of(index * size, size), size)


class Place:
    def __init__(self):
        self.zlo, self.x, self.core, self.y, self.zhi = (lax.axis_index(a) for a in AXES)
        turn = 1 - 2 * self.core
        self.chip = self.zlo * 4 + self.x
        self.share = 2 * self.y + self.zhi
        self.xf, self.xb, self.xo = (lax.rem(self.x + 4 + k, 4) for k in (turn, -turn, 2))
        self.yf, self.yb, self.yo = (lax.rem(self.y + 4 + k, 4) for k in (turn, -turn, 2))
        self.partner = {"core": 1 - self.core}
        self.far = {"zhi": 1 - self.zhi}


class Copies:
    def __init__(self, send, recv, local):
        self.send, self.recv, self.local = send, recv, local
        self.pushed, self.kept, self.count = [], [], 0

    def push(self, src, dst, device):
        index = self.count
        self.count += 1
        copy = pltpu.make_async_remote_copy(
            src, dst, self.send.at[index], self.recv.at[index], device_id=device, device_id_type=MESH
        )
        copy.start()
        self.pushed.append(copy)
        return index

    def got(self, index, region):
        pltpu.make_async_copy(region, region, self.recv.at[index]).wait()

    def keep(self, src, dst):
        copy = pltpu.make_async_copy(src, dst, self.local.at[len(self.kept)])
        copy.start()
        self.kept.append(copy)
        return copy

    def sent(self):
        for copy in self.pushed:
            copy.wait_send()


def greet(devices):
    barrier = pltpu.get_barrier_semaphore()
    for device in devices:
        pl.semaphore_signal(barrier, inc=1, device_id=device, device_id_type=MESH)
    pl.semaphore_wait(barrier, len(devices))


def x_start(copies, at, region, z):
    mine = region(z * 4 + at.x)
    return (
        copies.push(mine, mine, {"x": at.xf}),
        copies.push(mine, mine, {"x": at.xb}),
    )


def x_forward(copies, at, region, z, started):
    block = region(z * 4 + at.xb)
    copies.got(started[0], block)
    return copies.push(block, block, {"x": at.xf})


def x_rest(copies, at, region, z, started, forwarded):
    copies.got(started[1], region(z * 4 + at.xf))
    copies.got(forwarded, region(z * 4 + at.xo))


def scratch(pushes, locals_):
    return [
        pltpu.SemaphoreType.DMA((pushes,)),
        pltpu.SemaphoreType.DMA((pushes,)),
        pltpu.SemaphoreType.DMA((locals_,)),
    ]


def spread_kernel(tok, wq, wo, tok_all, wq_all, wo_all, send, recv, local):
    at = Place()
    copies = Copies(send, recv, local)
    zs = [lax.rem(at.zlo + k, 4) for k in (1, 3, 2)]
    zfrom = [lax.rem(at.zlo + 4 - k, 4) for k in (1, 3, 2)]
    greet(
        [at.partner, at.far, {"y": at.yf}, {"y": at.yb}, {"x": at.xf}, {"x": at.xb}]
        + [{"zlo": z} for z in zs]
    )

    def piece(share, half):
        return tok_all.at[at.core, share, pl.ds(32 * half, 32)]

    def wq_block(chip):
        return wq_all.at[:, aligned(chip, 192)]

    def wo_block(chip):
        return wo_all.at[:, chip]

    halves = (0, 1)
    source = [tok.at[pl.ds(32 * h, 32)] for h in halves]
    rows = wq_all.at[:, aligned(2 * at.chip + at.core, 96)]
    w_pair = copies.push(wq.at[:, :, aligned(1 - at.core, HEAD)], rows, at.partner)
    w_own = copies.keep(wq.at[:, :, aligned(at.core, HEAD)], rows)
    o_far = copies.push(wo, wo_all.at[at.zhi, at.chip], at.far)
    o_own = copies.keep(wo, wo_all.at[at.zhi, at.chip])
    far = [copies.push(source[h], piece(at.share, h), at.far) for h in halves]
    own_f = [copies.push(source[h], piece(at.share, h), {"y": at.yf}) for h in halves]
    own_b = [copies.push(source[h], piece(at.share, h), {"y": at.yb}) for h in halves]
    t_own = copies.keep(tok, tok_all.at[at.core, at.share])

    partner_rows = wq_all.at[:, aligned(2 * at.chip + 1 - at.core, 96)]
    copies.got(w_pair, partner_rows)
    w_own.wait()
    w_z = [copies.push(wq_block(at.chip), wq_block(at.chip), {"zlo": z}) for z in zs]
    w_x = [x_start(copies, at, wq_block, at.zlo)]
    copies.got(o_far, wo_all.at[1 - at.zhi, at.chip])
    o_own.wait()
    o_z = [copies.push(wo_block(at.chip), wo_block(at.chip), {"zlo": z}) for z in zs]
    o_x = [x_start(copies, at, wo_block, at.zlo)]

    shared = []

    def share_out(share):
        block = tok_all.at[at.core, share]
        shared.append((copies.push(block, block, at.partner), share))

    t_own.wait()
    share_out(at.share)
    back = 2 * at.yb + at.zhi
    ahead = 2 * at.yf + at.zhi
    beyond = 2 * at.yo + at.zhi
    fwd = []
    for h in halves:
        copies.got(own_f[h], piece(back, h))
        fwd.append(copies.push(piece(back, h), piece(back, h), {"y": at.yf}))
    w_f = [x_forward(copies, at, wq_block, at.zlo, w_x[0])]
    o_f = [x_forward(copies, at, wo_block, at.zlo, o_x[0])]
    share_out(back)
    for h in halves:
        copies.got(own_b[h], piece(ahead, h))
    share_out(ahead)
    far_share = 2 * at.y + 1 - at.zhi
    far_f, far_b = [], []
    for h in halves:
        copies.got(far[h], piece(far_share, h))
        far_f.append(copies.push(piece(far_share, h), piece(far_share, h), {"y": at.yf}))
        far_b.append(copies.push(piece(far_share, h), piece(far_share, h), {"y": at.yb}))
    share_out(far_share)
    for k in range(3):
        copies.got(w_z[k], wq_block(zfrom[k] * 4 + at.x))
        w_x.append(x_start(copies, at, wq_block, zfrom[k]))
        copies.got(o_z[k], wo_block(zfrom[k] * 4 + at.x))
        o_x.append(x_start(copies, at, wo_block, zfrom[k]))
    for h in halves:
        copies.got(fwd[h], piece(beyond, h))
    share_out(beyond)
    back, ahead, beyond = back + 1 - 2 * at.zhi, ahead + 1 - 2 * at.zhi, beyond + 1 - 2 * at.zhi
    w_f.append(x_forward(copies, at, wq_block, zfrom[0], w_x[1]))
    o_f.append(x_forward(copies, at, wo_block, zfrom[0], o_x[1]))
    fwd = []
    for h in halves:
        copies.got(far_f[h], piece(back, h))
        fwd.append(copies.push(piece(back, h), piece(back, h), {"y": at.yf}))
    share_out(back)
    for k in (1, 2):
        w_f.append(x_forward(copies, at, wq_block, zfrom[k], w_x[k + 1]))
        o_f.append(x_forward(copies, at, wo_block, zfrom[k], o_x[k + 1]))
    for h in halves:
        copies.got(far_b[h], piece(ahead, h))
    share_out(ahead)
    for h in halves:
        copies.got(fwd[h], piece(beyond, h))
    share_out(beyond)
    for k, z in enumerate([at.zlo] + zfrom):
        x_rest(copies, at, wq_block, z, w_x[k], w_f[k])
        x_rest(copies, at, wo_block, z, o_x[k], o_f[k])
    for index, share in shared:
        copies.got(index, tok_all.at[1 - at.core, share])
    copies.sent()


def attend_kernel(times, qkv, wo, out, wo_all, kv, top, total, mixed, send, recv, local):
    at = Place()
    copies = Copies(send, recv, local)
    zs = [lax.rem(at.zlo + k, 4) for k in (1, 3, 2)]
    zfrom = [lax.rem(at.zlo + 4 - k, 4) for k in (1, 3, 2)]
    greet(
        [at.partner, {"y": at.yf}, {"y": at.yb}, {"x": at.xf}, {"x": at.xb}]
        + [{"zlo": z} for z in zs]
    )

    def kv_block(chip):
        return kv.at[chip]

    def wo_block(y, core):
        return wo_all.at[pl.ds(2 * y, 2), :, core]

    def attend(chip):
        for t in range(2):
            rows = slice(512 * t, 512 * t + 512)
            own_time = times[2 * at.chip + t]
            scores = lax.dot_general(
                qkv[0, rows, :], kv[chip, 0], (((1,), (1,)), ((), ())), preferred_element_type=F32
            )
            seen = [times[2 * chip + j] <= own_time for j in (0, 1)]
            parts = [scores[:, :512], scores[:, 512:]]
            old = top[rows, :1]
            new = old
            for part, see in zip(parts, seen):
                new = jnp.maximum(
                    new, jnp.where(see, jnp.max(part, axis=1, keepdims=True), -1e30)
                )
            decay = jnp.exp2((old - new) * SCALE2)
            weights = [
                jnp.exp2((part - jnp.where(see, new, 1e30)) * SCALE2)
                for part, see in zip(parts, seen)
            ]
            lanes = total[rows, :] * decay
            for part in weights:
                for j in range(4):
                    lanes = lanes + part[:, 128 * j : 128 * j + 128]
            total[rows, :] = lanes
            top[rows, :] = jnp.broadcast_to(new, (512, 128))
            both = jnp.concatenate([part.astype(BF) for part in weights], axis=1)
            mixed[rows, :] = mixed[rows, :] * decay + jnp.dot(
                both, kv[chip, 1], preferred_element_type=F32
            )

    own = qkv.at[pl.ds(1, 2)]
    kv_z = [copies.push(own, kv_block(at.chip), {"zlo": zs[0]})]
    kv_x = [
        (
            copies.push(own, kv_block(at.chip), {"x": at.xf}),
            copies.push(own, kv_block(at.chip), {"x": at.xb}),
        )
    ]
    kv_own = copies.keep(own, kv_block(at.chip))
    wo_f = copies.push(wo, wo_block(at.y, at.core), {"y": at.yf})
    wo_b = copies.push(wo, wo_block(at.y, at.core), {"y": at.yb})
    wo_own = copies.keep(wo, wo_block(at.y, at.core))
    wo_p = [copies.push(wo, wo_block(at.y, at.core), at.partner)]
    top[...] = jnp.full_like(top, -1e30)
    total[...] = jnp.zeros_like(total)
    mixed[...] = jnp.zeros_like(mixed)
    kv_own.wait()
    attend(at.chip)
    order = [at.zlo] + zfrom
    wo_fwd = None
    for k in range(4):
        z = order[k]
        if k > 0:
            attend(z * 4 + at.x)
        forwarded = x_forward(copies, at, kv_block, z, kv_x[k])
        if k == 0:
            copies.pushed[0].wait_send()
            copies.pushed.pop(0)
            kv_z.append(copies.push(own, kv_block(at.chip), {"zlo": zs[1]}))
            second = copies.pushed.pop()
        if k < 3:
            copies.got(kv_z[k], kv_block(zfrom[k] * 4 + at.x))
            kv_x.append(x_start(copies, at, kv_block, zfrom[k]))
        if k == 0:
            second.wait_send()
            kv_z.append(copies.push(own, kv_block(at.chip), {"zlo": zs[2]}))
        attend(z * 4 + at.xb)
        copies.got(kv_x[k][1], kv_block(z * 4 + at.xf))
        attend(z * 4 + at.xf)
        if k == 1:
            block = wo_block(at.yb, at.core)
            copies.got(wo_f, block)
            wo_fwd = copies.push(block, block, {"y": at.yf})
            wo_p.append(copies.push(block, block, at.partner))
        if k == 2:
            block = wo_block(at.yf, at.core)
            copies.got(wo_b, block)
            wo_p.append(copies.push(block, block, at.partner))
        copies.got(forwarded, kv_block(z * 4 + at.xo))
        attend(z * 4 + at.xo)
    out[...] = (mixed[...] / jnp.sum(total[...], axis=1, keepdims=True)).astype(BF)
    block = wo_block(at.yo, at.core)
    copies.got(wo_fwd, block)
    wo_p.append(copies.push(block, block, at.partner))
    wo_own.wait()
    for index, y in zip(wo_p, (at.y, at.yb, at.yf, at.yo)):
        copies.got(index, wo_block(y, 1 - at.core))
    copies.sent()


def layer_kernel(
    attn,
    up,
    down,
    wo,
    tok,
    gain,
    conv,
    out,
    wo_here,
    rows,
    near,
    residual,
    window,
    gathered,
    ud,
    hidden,
    terms,
    relay,
    direct,
    summed,
    final,
    send,
    recv,
    local,
):
    at = Place()
    copies = Copies(send, recv, local)
    width = out.shape[1]
    deep = at.zhi * 4 + at.zlo
    z_steps = (1, 7, 2, 6, 3, 5, 4)
    zs = [lax.rem(deep + k, 8) for k in z_steps]
    order = [deep] + [lax.rem(deep + 8 - k, 8) for k in z_steps]
    peers = [(c, z, y) for z in (1, 0) for y in range(4) for c in (0, 1) if (c, z, y) != (0, 0, 0)]

    def peer(c, z, y, sign):
        return (
            lax.rem(at.core + c, 2),
            lax.rem(at.zhi + z, 2),
            lax.rem(at.y + 4 + sign * y, 4),
        )

    def named(place):
        return {"core": place[0], "zhi": place[1], "y": place[2]}

    def depth(z):
        return {"zhi": z // 4, "zlo": lax.rem(z, 4)}

    greet(
        [named(peer(*p, 1)) for p in peers]
        + [{"x": at.xf}, {"x": at.xb}]
        + [depth(z) for z in zs[:-1]]
    )

    def head_rows(head):
        return rows.at[:, aligned(head, HEAD)]

    def first_row(share):
        return jnp.clip(2 * share - 1, 0, 12)

    def needed(place):
        core, zhi, y = place
        return attn.at[core, pl.ds(pl.multiple_of(first_row(2 * y + zhi) * 32, 32), 128)]

    def ud_block(z, x):
        return ud.at[:, lax.rem(z, 4) * 4 + x, at.core, :, aligned(z // 4, 384)]

    def ud_lump(z, core):
        return ud.at[:, aligned(lax.rem(z, 4), 4), core, :, aligned(z // 4, 384)]

    head = 2 * at.share + at.core
    first = first_row(at.share)
    own_ud = [
        copies.keep(ref, ud.at[i, at.chip, at.core, :, aligned(at.zhi, 384)])
        for i, ref in enumerate((up, down))
    ]
    pushes = [copies.push(needed(peer(*p, 1)), head_rows(head), named(peer(*p, 1))) for p in peers]
    kept = copies.keep(needed((at.core, at.zhi, at.y)), head_rows(head))
    wo_copy = copies.keep(wo, wo_here)
    near_copy = copies.keep(
        tok.at[at.core, pl.ds(pl.multiple_of(first * 32, 32), 128)], near
    )
    for copy in own_ud:
        copy.wait()

    def z_push(k):
        block = ud_block(deep, at.x)
        return copies.push(block, block, depth(zs[k]))

    def x_push(z):
        block = ud_block(z, at.x)
        return (copies.push(block, block, {"x": at.xf}), copies.push(block, block, {"x": at.xb}))

    along_z = [z_push(k) for k in (0, 1)]
    opened, forwarded, lumps = [x_push(deep)], [], []

    def open_group(k):
        copies.got(along_z[k - 1], ud_block(order[k], at.x))
        opened.append(x_push(order[k]))

    def forward_group(k):
        block = ud_block(order[k], at.xb)
        copies.got(opened[k][0], block)
        forwarded.append(copies.push(block, block, {"x": at.xf}))

    def close_group(k):
        copies.got(opened[k][1], ud_block(order[k], at.xf))
        copies.got(forwarded[k], ud_block(order[k], at.xo))
        lump = ud_lump(order[k], at.core)
        lumps.append(copies.push(lump, lump, at.partner))

    shift = 2 * at.share - 1 - first
    for r in (1, 4):
        window[r] = jnp.zeros(window.shape[1:], F32)
    near_copy.wait()
    wo_copy.wait()
    kept.wait()
    for index, p in zip(pushes, peers):
        core, zhi, y = peer(*p, -1)
        copies.got(index, head_rows(2 * (2 * y + zhi) + core))
    along_z.extend(z_push(k) for k in range(2, 7))
    open_group(1)
    open_group(2)
    forward_group(0)

    def project(n, carry):
        columns = aligned(n, 256)
        acc = near[:, columns].astype(F32)
        for s in range(8):
            acc = acc + lax.dot_general(
                rows[:, 256 * s : 256 * s + 256],
                wo_here[s, columns, :],
                (((1,), (1,)), ((), ())),
                preferred_element_type=F32,
            )
        residual[:, columns] = acc
        return carry

    lax.fori_loop(0, 12, project, 0)
    forward_group(1)
    open_group(3)
    open_group(4)
    for r in range(4):
        row = residual[32 * r : 32 * r + 32, :]
        mean_square = jnp.mean(row * row, axis=1, keepdims=True)
        normed = row * lax.rsqrt(mean_square + 1e-06) * gain[...].astype(F32)
        window[1 + r - shift] = normed.astype(BF).astype(F32)
    close_group(0)
    forward_group(2)
    line = lax.broadcasted_iota(jnp.int32, (32, 512), 0)

    def convolve(j):
        def tile(n, carry):
            columns = aligned(n, 512)
            sums = [jnp.zeros((32, 512), F32)] * 3
            for a in range(3):
                taps = conv[a, :, columns].astype(F32)
                values = window[1 + j + a, :, columns]
                for b in range(3):
                    sums[b] = sums[b] + values * taps[b : b + 1, :]
            before = jnp.where(line == 0, 0.0, pltpu.roll(sums[0], 1, 0))
            after = jnp.where(line == 31, 0.0, pltpu.roll(sums[2], 31, 0))
            gathered[aligned(2 * at.y + j, 32), columns] = (before + sums[1] + after).astype(BF)
            return carry

        lax.fori_loop(0, width // 512, tile, 0)

    def token_piece(y, h):
        return gathered.at[aligned(2 * y + h, 32)]

    ahead, behind = [], []
    for h in (0, 1):
        convolve(h)
        piece = token_piece(at.y, h)
        ahead.append(copies.push(piece, piece, {"y": at.yf}))
        behind.append(copies.push(piece, piece, {"y": at.yb}))
    open_group(5)
    open_group(6)
    close_group(1)
    forward_group(3)
    token_fwd = []
    for h in (0, 1):
        piece = token_piece(at.yb, h)
        copies.got(ahead[h], piece)
        token_fwd.append(copies.push(piece, piece, {"y": at.yf}))
    open_group(7)
    close_group(2)
    for k in (4, 5, 6, 7):
        forward_group(k)
        close_group(k - 1)
    close_group(7)
    for h in (0, 1):
        copies.got(behind[h], token_piece(at.yf, h))
        copies.got(token_fwd[h], token_piece(at.yo, h))
    for index, z in zip(lumps, order):
        copies.got(index, ud_lump(z, 1 - at.core))

    for n in range(3):
        columns = slice(256 * n, 256 * n + 256)
        value = jnp.dot(
            gathered[...],
            ud[0, :, :, :, columns].reshape(width, 256),
            preferred_element_type=F32,
        )
        hidden[:, columns] = jax.nn.gelu(value).astype(BF)

    chunk = width // 4

    def columns_of(q):
        return slice(chunk * q, chunk * q + chunk)

    def term(y, q):
        return terms.at[aligned(y, 64), pl.ds(chunk * q, chunk)]

    def strip(ref, q):
        return ref.at[:, pl.ds(chunk * q, chunk)]

    relays, directs, finals = [], [], []

    def pass_on(q):
        copies.got(relays[q], strip(relay, q))
        columns = columns_of(q)
        summed[:, columns] = (
            terms[aligned(at.yf, 64), columns].astype(F32) + relay[:, columns].astype(F32)
        ).astype(BF)
        finals.append(copies.push(strip(summed, q), strip(final, q), {"y": at.yf}))

    for q in range(4):
        terms[:, columns_of(q)] = lax.dot_general(
            hidden[...],
            ud[1, 4 * q : 4 * q + 4].reshape(chunk, chunk),
            (((1,), (1,)), ((), ())),
            preferred_element_type=F32,
        ).astype(BF)
        relays.append(copies.push(term(at.yo, q), strip(relay, q), {"y": at.yf}))
        directs.append(copies.push(term(at.yb, q), strip(direct, q), {"y": at.yb}))
        if q > 0:
            pass_on(q - 1)
    pass_on(3)
    own_rows = pl.ds(pl.multiple_of((1 + shift) * 32, 32), 64)
    for q in range(4):
        columns = columns_of(q)
        copies.got(directs[q], strip(direct, q))
        partial = (
            residual[own_rows, columns]
            + terms[aligned(at.y, 64), columns].astype(F32)
            + direct[:, columns].astype(F32)
        )
        copies.got(finals[q], strip(final, q))
        out[:, columns] = (partial + final[:, columns].astype(F32)).astype(BF)
    copies.sent()


def remote(collective_id, megabytes=32):
    return pltpu.CompilerParams(
        collective_id=collective_id, has_side_effects=True, vmem_limit_bytes=megabytes << 20
    )


def shape(*dims, dtype=BF):
    return jax.ShapeDtypeStruct(dims, dtype)


def shards(
    tokens, frame_time, qkv_weight, out_weight, norm_gain, conv_weight, up_weight, down_weight
):
    width = tokens.shape[3]
    tok_all, wq_all, wo_part = pl.pallas_call(
        spread_kernel,
        out_shape=(shape(2, 8, 64, width), shape(3, width, HEAD), shape(2, 16, 96, 256)),
        in_specs=[ANY] * 3,
        out_specs=(ANY,) * 3,
        scratch_shapes=scratch(64, 4),
        compiler_params=remote(1),
    )(tokens.reshape(64, width), qkv_weight, out_weight.T)
    qkv = jnp.einsum(
        "td,idh->ith", tok_all.reshape(1024, width), wq_all, preferred_element_type=F32
    ).astype(BF)
    attn, wo_all = pl.pallas_call(
        attend_kernel,
        out_shape=(shape(1024, HEAD), shape(8, 16, 2, 96, 256)),
        in_specs=[SMEM, VMEM, ANY],
        out_specs=(VMEM, ANY),
        scratch_shapes=[
            pltpu.VMEM((16, 2, 1024, HEAD), BF),
            pltpu.VMEM((1024, HEAD), F32),
            pltpu.VMEM((1024, HEAD), F32),
            pltpu.VMEM((1024, HEAD), F32),
        ]
        + scratch(24, 2),
        compiler_params=remote(2, 40),
    )(frame_time, qkv, wo_part)
    result = pl.pallas_call(
        layer_kernel,
        out_shape=shape(64, width),
        in_specs=[ANY] * 5 + [VMEM] * 2,
        out_specs=VMEM,
        scratch_shapes=[
            pltpu.VMEM((8, width, 256), BF),
            pltpu.VMEM((128, 16 * HEAD), BF),
            pltpu.VMEM((128, width), BF),
            pltpu.VMEM((128, width), F32),
            pltpu.VMEM((6, 32, width), F32),
            pltpu.VMEM((256, width), BF),
            pltpu.VMEM((2, 16, 2, 96, 768), BF),
            pltpu.VMEM((256, 768), BF),
            pltpu.VMEM((256, width), BF),
        ]
        + [pltpu.VMEM((64, width), BF)] * 4
        + scratch(80, 5),
        compiler_params=remote(3, 56),
    )(
        attn.reshape(2, 512, HEAD),
        up_weight,
        down_weight.T,
        wo_all.reshape(8, width, 256),
        tok_all.reshape(2, 512, width),
        norm_gain.reshape(1, width),
        conv_weight,
    )
    return result.reshape(1, 2, 32, width)


def solution(mesh):
    fine = Mesh(mesh.devices.reshape(4, 4, 2, 4, 2), AXES)
    frame, fsdp = ("zlo", "x", "core"), ("y", "zhi")
    placed = (
        P(frame, fsdp, None, None),
        P(),
        P(None, frame, fsdp),
        P(fsdp, frame),
        P(),
        P(),
        P(frame, fsdp),
        P(fsdp, frame),
    )
    return jax.shard_map(
        shards,
        mesh=fine,
        in_specs=placed,
        out_specs=P(frame, fsdp, None, None),
        check_vma=False,
    )
```

```python
import math

import jax
import jax.numpy as jnp
from jax import lax
from jax.experimental import pallas as pl
from jax.experimental.pallas import tpu as pltpu
from jax.sharding import Mesh
from jax.sharding import PartitionSpec as P

HEAD = 128
MESH = pl.DeviceIdType.MESH
BF = jnp.bfloat16
F32 = jnp.float32
AXES = ("zlo", "x", "core", "y", "zhi")
ANY = pl.BlockSpec(memory_space=pl.ANY)
VMEM = pl.BlockSpec(memory_space=pltpu.VMEM)
SMEM = pl.BlockSpec(memory_space=pltpu.SMEM)
SCALE2 = math.log2(math.e) / math.sqrt(HEAD)


def aligned(index, size):
    return pl.ds(pl.multiple_of(index * size, size), size)


class Place:
    def __init__(self):
        self.zlo, self.x, self.core, self.y, self.zhi = (lax.axis_index(a) for a in AXES)
        turn = 1 - 2 * self.core
        self.chip = self.zlo * 4 + self.x
        self.share = 2 * self.y + self.zhi
        self.xf, self.xb, self.xo = (lax.rem(self.x + 4 + k, 4) for k in (turn, -turn, 2))
        self.yf, self.yb, self.yo = (lax.rem(self.y + 4 + k, 4) for k in (turn, -turn, 2))
        self.partner = {"core": 1 - self.core}
        self.side = self.x // 2
        self.xs = self.x + 1 - 2 * lax.rem(self.x, 2)
        self.xp = 3 - self.x
        self.zq = self.zlo + 1 - 2 * lax.rem(self.zlo, 2)
        self.far = {"zhi": 1 - self.zhi}


class Copies:
    def __init__(self, send, recv, local):
        self.send, self.recv, self.local = send, recv, local
        self.pushed, self.kept, self.count = {}, 0, 0

    def reserve(self):
        self.count += 1
        return self.count - 1

    def push(self, src, dst, device, lands=None, when=None):
        index = self.reserve()
        arrives = self.recv.at[index if lands is None else lands]
        copy = pltpu.make_async_remote_copy(
            src, dst, self.send.at[index], arrives, device_id=device, device_id_type=MESH
        )
        if when is None:
            copy.start()
        else:
            pl.when(when)(copy.start)
        self.pushed[index] = (copy, when)
        return index

    def hand(self, src, dst, device, here, lands):
        copy = pltpu.make_async_copy(src, dst, self.recv.at[lands])
        pl.when(here)(copy.start)
        self.push(src, dst, device, lands, jnp.logical_not(here))

    def got(self, index, region):
        pltpu.make_async_copy(region, region, self.recv.at[index]).wait()

    def keep(self, src, dst):
        copy = pltpu.make_async_copy(src, dst, self.local.at[self.kept])
        copy.start()
        self.kept += 1
        return copy

    def left(self, index):
        copy, when = self.pushed.pop(index)
        if when is None:
            copy.wait_send()
        else:
            pl.when(when)(copy.wait_send)

    def sent(self):
        for index in list(self.pushed):
            self.left(index)


def greet(devices):
    barrier = pltpu.get_barrier_semaphore()
    for device in devices:
        pl.semaphore_signal(barrier, inc=1, device_id=device, device_id_type=MESH)
    pl.semaphore_wait(barrier, len(devices))


def x_start(copies, at, region, z):
    mine = region(z * 4 + at.x)
    return (
        copies.push(mine, mine, {"x": at.xf}),
        copies.push(mine, mine, {"x": at.xb}),
    )


def x_forward(copies, at, region, z, started):
    block = region(z * 4 + at.xb)
    copies.got(started[0], block)
    return copies.push(block, block, {"x": at.xf})


def x_rest(copies, at, region, z, started, forwarded):
    copies.got(started[1], region(z * 4 + at.xf))
    copies.got(forwarded, region(z * 4 + at.xo))


def scratch(pushes, locals_):
    return [
        pltpu.SemaphoreType.DMA((pushes,)),
        pltpu.SemaphoreType.DMA((pushes,)),
        pltpu.SemaphoreType.DMA((locals_,)),
    ]


def layer_kernel(
    times,
    tokens,
    wq,
    wo,
    up,
    down,
    gain,
    conv,
    out,
    tok,
    wq_here,
    stage,
    queries,
    kv,
    top,
    total,
    mixed,
    attn,
    wo_here,
    rows,
    residual,
    window,
    gathered,
    ud,
    hidden,
    terms,
    relay,
    direct,
    summed,
    final,
    send,
    recv,
    local,
):
    at = Place()
    copies = Copies(send, recv, local)
    width = out.shape[1]
    deep = at.zhi * 4 + at.zlo
    z_steps = (1, 7, 2, 6, 3, 5, 4)
    deep_to = [lax.rem(deep + k, 8) for k in z_steps]
    order = [deep] + [lax.rem(deep + 8 - k, 8) for k in z_steps]
    zs = [lax.rem(at.zlo + k, 4) for k in (1, 3, 2)]
    zfrom = [at.zlo] + [lax.rem(at.zlo + 4 - k, 4) for k in (1, 3, 2)]
    peers = [(c, z, y) for z in (1, 0) for y in range(4) for c in (0, 1) if (c, z, y) != (0, 0, 0)]
    halves = (0, 1)

    def peer(c, z, y, sign):
        return (
            lax.rem(at.core + c, 2),
            lax.rem(at.zhi + z, 2),
            lax.rem(at.y + 4 + sign * y, 4),
        )

    def named(place):
        return {"core": place[0], "zhi": place[1], "y": place[2]}

    def depth(z):
        return {"zhi": z // 4, "zlo": lax.rem(z, 4)}

    greet(
        [named(peer(*p, 1)) for p in peers]
        + [{"x": at.xp, **named(peer(*p, 1))} for p in peers + [(0, 0, 0)]]
        + [{"x": at.xs}]
        + [depth(z) for z in deep_to[:-1]]
    )


    def piece(share, half):
        return tok.at[at.core, pl.ds(pl.multiple_of(share * 64 + half * 32, 32), 32)]

    def share_block(core, share):
        return tok.at[core, aligned(share, 64)]

    def wq_block(chip):
        return wq_here.at[aligned(chip, 192)]

    def wo_block(chip):
        return wo_here.at[pl.ds(2 * at.y, 2), chip, at.core]

    def wo_plane(y, core):
        return wo_here.at[pl.ds(2 * y, 2), :, core]

    def kv_block(chip):
        return kv.at[chip]

    source = [tokens.at[pl.ds(32 * h, 32)] for h in halves]

    def wq_piece(core, i):
        return wq_here.at[aligned(2 * at.chip + core, 96), pl.ds(HEAD * i, HEAD)]

    far = []
    w_pair = [
        copies.push(
            wq.at[i, :, aligned(1 - at.core, HEAD)], wq_piece(at.core, i), at.partner
        )
        for i in range(3)
    ]
    w_own = [
        copies.keep(wq.at[i, :, aligned(at.core, HEAD)], wq_piece(at.core, i)) for i in range(3)
    ]
    own_f = [copies.push(source[h], piece(at.share, h), {"y": at.yf}) for h in halves]
    own_b = [copies.push(source[h], piece(at.share, h), {"y": at.yb}) for h in halves]
    t_own = copies.keep(tokens, share_block(at.core, at.share))
    o_own = copies.keep(wo, wo_here.at[at.share, at.chip, at.core])
    own_ud = [
        copies.keep(ref, ud.at[i, at.chip, at.core, :, aligned(at.zhi, 384)])
        for i, ref in enumerate((up, down))
    ]
    shared = []

    def share_out(share):
        block = share_block(at.core, share)
        shared.append((copies.push(block, block, at.partner), share))

    for i in range(3):
        w_own[i].wait()
        copies.got(w_pair[i], wq_piece(1 - at.core, i))
    w_z = [copies.push(wq_block(at.chip), wq_block(at.chip), {"zlo": z}) for z in zs]
    w_x = [x_start(copies, at, wq_block, at.zlo)]
    far.append(copies.push(source[0], piece(at.share, 0), at.far))
    far.append(copies.push(source[1], piece(at.share, 1), at.far))
    o_far = copies.push(wo, wo_here.at[at.share, at.chip, at.core], at.far)
    t_own.wait()
    share_out(at.share)
    far_share = 2 * at.y + 1 - at.zhi
    near_ring = [2 * y + at.zhi for y in (at.yb, at.yf, at.yo)]
    far_ring = [2 * y + 1 - at.zhi for y in (at.yb, at.yf, at.yo)]
    fwd, far_f, far_b = [], [], []

    def pass_tokens(index, share, half):
        block = piece(share, half)
        copies.got(index, block)
        return copies.push(block, block, {"y": at.yf})

    def spread_far(h):
        block = piece(far_share, h)
        copies.got(far[h], block)
        far_f.append(copies.push(block, block, {"y": at.yf}))
        far_b.append(copies.push(block, block, {"y": at.yb}))

    w_f = []

    def w_open(k):
        copies.got(w_z[k - 1], wq_block(zfrom[k] * 4 + at.x))
        w_x.append(x_start(copies, at, wq_block, zfrom[k]))

    def w_forward(k):
        w_f.append(x_forward(copies, at, wq_block, zfrom[k], w_x[k]))

    fwd.append(pass_tokens(own_f[0], near_ring[0], 0))
    w_forward(0)
    w_open(1)
    fwd.append(pass_tokens(own_f[1], near_ring[0], 1))
    share_out(near_ring[0])
    w_forward(1)
    w_open(2)
    for h in halves:
        copies.got(own_b[h], piece(near_ring[1], h))
    share_out(near_ring[1])
    w_open(3)
    w_forward(2)
    spread_far(0)
    for h in halves:
        copies.got(fwd[h], piece(near_ring[2], h))
    share_out(near_ring[2])
    w_forward(3)
    spread_far(1)
    share_out(far_share)
    o_own.wait()
    copies.got(o_far, wo_here.at[far_share, at.chip, at.core])
    o_z = [copies.push(wo_block(at.chip), wo_block(at.chip), {"zlo": z}) for z in zs]
    o_x = [x_start(copies, at, wo_block, at.zlo)]
    fwd = []
    for h in halves:
        fwd.append(pass_tokens(far_f[h], far_ring[0], h))
    share_out(far_ring[0])
    for h in halves:
        copies.got(far_b[h], piece(far_ring[1], h))
    share_out(far_ring[1])
    o_f = [x_forward(copies, at, wo_block, at.zlo, o_x[0])]
    for h in halves:
        copies.got(fwd[h], piece(far_ring[2], h))
    share_out(far_ring[2])
    for k in range(4):
        x_rest(copies, at, wq_block, zfrom[k], w_x[k], w_f[k])
    for index, share in shared:
        copies.got(index, share_block(1 - at.core, share))


    native = at.core == at.side
    across = {"x": at.xp, "core": 1 - at.core}
    px = at.core * at.side + (1 - at.core) * (1 - at.side)
    px = px * at.x + (1 - px) * at.xp
    pxs = px + 1 - 2 * lax.rem(px, 2)
    held = at.zlo * 4 + px
    inner = jnp.logical_or(at.zlo == 1, at.zlo == 2)
    zi = 3 - at.zlo
    zsrc = [at.zlo, at.zq, 2 - at.zlo // 2, 3 - 3 * (at.zlo // 2)]
    handed = [copies.reserve() for _ in range(3)]
    for t in range(2):
        part = pl.ds(512 * t, 512)
        both = jnp.dot(tok[t], wq_here[:, HEAD:], preferred_element_type=F32).astype(BF)
        stage[1, part, :] = both[:, :HEAD]
        stage[2, part, :] = both[:, HEAD:]
        copies.hand(
            stage.at[pl.ds(1, 2), part], kv.at[at.chip, :, part], across, native, handed[t]
        )
    for t in range(2):
        stage[0, pl.ds(512 * t, 512), :] = jnp.dot(
            tok[t], wq_here[:, :HEAD], preferred_element_type=F32
        ).astype(BF)
    copies.hand(stage.at[0], queries, across, native, handed[2])
    top[...] = jnp.full_like(top, -1e30)
    total[...] = jnp.zeros_like(total)
    mixed[...] = jnp.zeros_like(mixed)
    for t in range(2):
        copies.got(handed[t], kv.at[held, :, pl.ds(512 * t, 512)])

    def attend(chip):
        for t in range(2):
            part_rows = slice(512 * t, 512 * t + 512)
            own_time = times[2 * held + t]
            scores = lax.dot_general(
                queries[part_rows, :],
                kv[chip, 0],
                (((1,), (1,)), ((), ())),
                preferred_element_type=F32,
            )
            seen = [times[2 * chip + j] <= own_time for j in (0, 1)]
            parts = [scores[:, :512], scores[:, 512:]]
            old = top[part_rows, :1]
            new = old
            for part, see in zip(parts, seen):
                new = jnp.maximum(
                    new, jnp.where(see, jnp.max(part, axis=1, keepdims=True), -1e30)
                )
            decay = jnp.exp2((old - new) * SCALE2)
            weights = [
                jnp.exp2((part - jnp.where(see, new, 1e30)) * SCALE2)
                for part, see in zip(parts, seen)
            ]
            lanes = total[part_rows, :] * decay
            for part in weights:
                for j in range(4):
                    lanes = lanes + part[:, 128 * j : 128 * j + 128]
            total[part_rows, :] = lanes
            top[part_rows, :] = jnp.broadcast_to(new, (512, 128))
            both = jnp.concatenate([part.astype(BF) for part in weights], axis=1)
            mixed[part_rows, :] = mixed[part_rows, :] * decay + jnp.dot(
                both, kv[chip, 1], preferred_element_type=F32
            )

    lands = [copies.reserve() for _ in range(3)]
    beside, columns_over, beside_over = [], [], []

    def column(k, x):
        return kv_block(zsrc[k] * 4 + x)

    def kv_open(k):
        block = column(k, px)
        if k > 0:
            copies.got(lands[k - 1], block)
        beside.append(copies.push(block, block, {"x": at.xs}))
        if k == 0:
            copies.push(block, block, {"zlo": at.zq}, lands[0])
            copies.push(block, block, {"zlo": zi}, lands[1], inner)
        if k == 1:
            copies.push(block, block, {"zlo": zi}, lands[2], inner)
        if k > 1:
            copies.push(block, block, {"zlo": at.zq}, lands[k - 1], inner)
        columns_over.append(copies.push(block, block, at.partner))

    def kv_beside(k):
        block = column(k, pxs)
        copies.got(beside[k], block)
        beside_over.append(copies.push(block, block, at.partner))

    def attend_column(k):
        attend(zsrc[k] * 4 + px)

    def attend_beside(k):
        attend(zsrc[k] * 4 + pxs)

    def attend_column_over(k):
        copies.got(columns_over[k], column(k, 3 - px))
        attend(zsrc[k] * 4 + 3 - px)

    def attend_beside_over(k):
        copies.got(beside_over[k], column(k, 3 - pxs))
        attend(zsrc[k] * 4 + 3 - pxs)

    def ud_block(z, x):
        return ud.at[:, lax.rem(z, 4) * 4 + x, at.core, :, aligned(z // 4, 384)]

    def ud_lump(z, core):
        return ud.at[:, aligned(lax.rem(z, 4), 4), core, :, aligned(z // 4, 384)]

    def x_push(z):
        block = ud_block(z, at.x)
        return (copies.push(block, block, {"x": at.xf}), copies.push(block, block, {"x": at.xb}))

    kv_open(0)
    for k in (1, 2, 3):
        copies.got(o_z[k - 1], wo_block(zfrom[k] * 4 + at.x))
        o_x.append(x_start(copies, at, wo_block, zfrom[k]))
    copies.got(handed[2], queries)
    attend_column(0)
    attend_column_over(0)
    for k in (1, 2, 3):
        o_f.append(x_forward(copies, at, wo_block, zfrom[k], o_x[k]))
    kv_open(1)
    kv_beside(0)
    attend_beside(0)
    for k in range(4):
        x_rest(copies, at, wo_block, zfrom[k], o_x[k], o_f[k])
    plane = wo_plane(at.y, at.core)
    wo_f = copies.push(plane, plane, {"y": at.yf})
    wo_b = copies.push(plane, plane, {"y": at.yb})
    wo_p = [copies.push(plane, plane, at.partner)]
    attend_column(1)
    attend_column_over(1)
    attend_beside_over(0)
    kv_open(2)
    kv_beside(1)
    attend_beside(1)
    attend_column(2)
    attend_column_over(2)
    attend_beside_over(1)
    kv_open(3)
    for copy in own_ud:
        copy.wait()
    block = ud_block(deep, at.x)
    along_z = [copies.push(block, block, depth(z)) for z in deep_to]
    kv_beside(2)
    attend_beside(2)
    attend_column(3)
    attend_column_over(3)
    attend_beside_over(2)
    kv_beside(3)
    attend_beside(3)
    attend_beside_over(3)
    plane = wo_plane(at.yb, at.core)
    copies.got(wo_f, plane)
    wo_fwd = copies.push(plane, plane, {"y": at.yf})
    wo_p.append(copies.push(plane, plane, at.partner))
    plane = wo_plane(at.yf, at.core)
    copies.got(wo_b, plane)
    wo_p.append(copies.push(plane, plane, at.partner))
    for t in range(2):
        part_rows = slice(512 * t, 512 * t + 512)
        attn[t] = (
            mixed[part_rows, :] / jnp.sum(total[part_rows, :], axis=1, keepdims=True)
        ).astype(BF)


    def head_rows(head):
        return rows.at[:, aligned(head, HEAD)]

    def first_row(share):
        return jnp.clip(2 * share - 1, 0, 12)

    def needed(place):
        core, zhi, y = place
        return attn.at[core, pl.ds(pl.multiple_of(first_row(2 * y + zhi) * 32, 32), 128)]

    head = 2 * at.share + at.side
    first = first_row(at.share)
    role = at.core + at.side - 2 * at.core * at.side
    places = [(z, y) for z in (1, 0) for y in range(4)]
    arrivals = []
    for z, y in places:
        base = copies.reserve()
        copies.reserve()
        arrivals.append(base)
        for c in (0, 1):
            _, zhi, y_to = peer(0, z, y, 1)
            goal = (lax.rem(at.core + c, 2), zhi, y_to)
            device = {"x": px, **named(goal)}
            if (c, z, y) == (0, 0, 0):
                copies.hand(needed(goal), head_rows(head), device, native, base + role)
            else:
                copies.push(needed(goal), head_rows(head), device, base + role)
    opened, forwarded, lumps = [x_push(deep)], [], []

    def open_group(k):
        copies.got(along_z[k - 1], ud_block(order[k], at.x))
        opened.append(x_push(order[k]))

    def forward_group(k):
        block = ud_block(order[k], at.xb)
        copies.got(opened[k][0], block)
        forwarded.append(copies.push(block, block, {"x": at.xf}))

    def close_group(k):
        copies.got(opened[k][1], ud_block(order[k], at.xf))
        copies.got(forwarded[k], ud_block(order[k], at.xo))
        lump = ud_lump(order[k], at.core)
        lumps.append(copies.push(lump, lump, at.partner))

    shift = 2 * at.share - 1 - first
    for r in (1, 4):
        window[r] = jnp.zeros(window.shape[1:], F32)
    for k in (1, 2, 3):
        open_group(k)
    forward_group(0)
    plane = wo_plane(at.yo, at.core)
    copies.got(wo_fwd, plane)
    wo_p.append(copies.push(plane, plane, at.partner))
    for base, (z, y) in zip(arrivals, places):
        _, zhi, y_from = peer(0, z, y, -1)
        whose = 2 * (2 * y_from + zhi)
        copies.got(base, head_rows(whose + at.side))
        copies.got(base + 1, head_rows(whose + 1 - at.side))
    for index, y in zip(wo_p, (at.y, at.yb, at.yf, at.yo)):
        copies.got(index, wo_plane(y, 1 - at.core))
    for k in (4, 5):
        open_group(k)
    forward_group(1)
    near_rows = pl.ds(pl.multiple_of(first * 32, 32), 128)

    def project(n, carry):
        columns = aligned(n, 768)
        acc = tok[at.core, near_rows, columns].astype(F32)
        for s in range(8):
            acc = acc + lax.dot_general(
                rows[:, 256 * s : 256 * s + 256],
                wo_here[s, pl.ds(4 * n, 4)].reshape(768, 256),
                (((1,), (1,)), ((), ())),
                preferred_element_type=F32,
            )
        residual[:, columns] = acc
        return carry

    lax.fori_loop(0, 4, project, 0)
    for k in (6, 7):
        open_group(k)
    forward_group(2)
    close_group(0)
    forward_group(3)
    for r in range(4):
        row = residual[32 * r : 32 * r + 32, :]
        mean_square = jnp.mean(row * row, axis=1, keepdims=True)
        normed = row * lax.rsqrt(mean_square + 1e-06) * gain[...].astype(F32)
        window[1 + r - shift] = normed.astype(BF).astype(F32)
    close_group(1)
    line = lax.broadcasted_iota(jnp.int32, (32, 512), 0)

    def convolve(j):
        def tile(n, carry):
            columns = aligned(n, 512)
            sums = [jnp.zeros((32, 512), F32)] * 3
            for a in range(3):
                taps = conv[a, :, columns].astype(F32)
                values = window[1 + j + a, :, columns]
                for b in range(3):
                    sums[b] = sums[b] + values * taps[b : b + 1, :]
            before = jnp.where(line == 0, 0.0, pltpu.roll(sums[0], 1, 0))
            after = jnp.where(line == 31, 0.0, pltpu.roll(sums[2], 31, 0))
            gathered[aligned(2 * at.y + j, 32), columns] = (before + sums[1] + after).astype(BF)
            return carry

        lax.fori_loop(0, width // 512, tile, 0)

    def token_piece(y, h):
        return gathered.at[aligned(2 * y + h, 32)]

    ahead, behind = [], []
    for h in (0, 1):
        convolve(h)
        piece = token_piece(at.y, h)
        ahead.append(copies.push(piece, piece, {"y": at.yf}))
        behind.append(copies.push(piece, piece, {"y": at.yb}))
    forward_group(4)
    close_group(2)
    token_fwd = []
    for h in (0, 1):
        piece = token_piece(at.yb, h)
        copies.got(ahead[h], piece)
        token_fwd.append(copies.push(piece, piece, {"y": at.yf}))
    close_group(3)
    for k in (5, 6, 7):
        forward_group(k)
        close_group(k - 1)
    close_group(7)
    for h in (0, 1):
        copies.got(behind[h], token_piece(at.yf, h))
        copies.got(token_fwd[h], token_piece(at.yo, h))
    for index, z in zip(lumps, order):
        copies.got(index, ud_lump(z, 1 - at.core))

    for n in range(3):
        columns = slice(256 * n, 256 * n + 256)
        value = jnp.dot(
            gathered[...],
            ud[0, :, :, :, columns].reshape(width, 256),
            preferred_element_type=F32,
        )
        hidden[:, columns] = jax.nn.gelu(value).astype(BF)

    chunk = width // 4

    def columns_of(q):
        return slice(chunk * q, chunk * q + chunk)

    def term(y, q):
        return terms.at[aligned(y, 64), pl.ds(chunk * q, chunk)]

    def strip(ref, q):
        return ref.at[:, pl.ds(chunk * q, chunk)]

    relays, directs, finals = [], [], []

    def pass_on(q):
        copies.got(relays[q], strip(relay, q))
        columns = columns_of(q)
        summed[:, columns] = (
            terms[aligned(at.yf, 64), columns].astype(F32) + relay[:, columns].astype(F32)
        ).astype(BF)
        finals.append(copies.push(strip(summed, q), strip(final, q), {"y": at.yf}))

    for q in range(4):
        terms[:, columns_of(q)] = lax.dot_general(
            hidden[...],
            ud[1, 4 * q : 4 * q + 4].reshape(chunk, chunk),
            (((1,), (1,)), ((), ())),
            preferred_element_type=F32,
        ).astype(BF)
        relays.append(copies.push(term(at.yo, q), strip(relay, q), {"y": at.yf}))
        directs.append(copies.push(term(at.yb, q), strip(direct, q), {"y": at.yb}))
        if q > 0:
            pass_on(q - 1)
    pass_on(3)
    own_rows = pl.ds(pl.multiple_of((1 + shift) * 32, 32), 64)
    for q in range(4):
        columns = columns_of(q)
        copies.got(directs[q], strip(direct, q))
        partial = (
            residual[own_rows, columns]
            + terms[aligned(at.y, 64), columns].astype(F32)
            + direct[:, columns].astype(F32)
        )
        copies.got(finals[q], strip(final, q))
        out[:, columns] = (partial + final[:, columns].astype(F32)).astype(BF)
    copies.sent()


def remote(collective_id, megabytes=32):
    return pltpu.CompilerParams(
        collective_id=collective_id, has_side_effects=True, vmem_limit_bytes=megabytes << 20
    )


def shape(*dims, dtype=BF):
    return jax.ShapeDtypeStruct(dims, dtype)


def shards(
    tokens, frame_time, qkv_weight, out_weight, norm_gain, conv_weight, up_weight, down_weight
):
    width = tokens.shape[3]
    result = pl.pallas_call(
        layer_kernel,
        out_shape=shape(64, width),
        in_specs=[SMEM] + [ANY] * 5 + [VMEM] * 2,
        out_specs=VMEM,
        scratch_shapes=[
            pltpu.VMEM((2, 512, width), BF),
            pltpu.VMEM((width, 3 * HEAD), BF),
            pltpu.VMEM((3, 1024, HEAD), BF),
            pltpu.VMEM((1024, HEAD), BF),
            pltpu.VMEM((16, 2, 1024, HEAD), BF),
            pltpu.VMEM((1024, HEAD), F32),
            pltpu.VMEM((1024, HEAD), F32),
            pltpu.VMEM((1024, HEAD), F32),
            pltpu.VMEM((2, 512, HEAD), BF),
            pltpu.VMEM((8, 16, 2, 96, 256), BF),
            pltpu.VMEM((128, 16 * HEAD), BF),
            pltpu.VMEM((128, width), F32),
            pltpu.VMEM((6, 32, width), F32),
            pltpu.VMEM((256, width), BF),
            pltpu.VMEM((2, 16, 2, 96, 768), BF),
            pltpu.VMEM((256, 768), BF),
            pltpu.VMEM((256, width), BF),
        ]
        + [pltpu.VMEM((64, width), BF)] * 4
        + scratch(224, 8),
        compiler_params=remote(1, 60),
    )(
        frame_time,
        tokens.reshape(64, width),
        qkv_weight,
        out_weight.T,
        up_weight,
        down_weight.T,
        norm_gain.reshape(1, width),
        conv_weight,
    )
    return result.reshape(1, 2, 32, width)


def solution(mesh):
    fine = Mesh(mesh.devices.reshape(4, 4, 2, 4, 2), AXES)
    frame, fsdp = ("zlo", "x", "core"), ("y", "zhi")
    placed = (
        P(frame, fsdp, None, None),
        P(),
        P(None, frame, fsdp),
        P(fsdp, frame),
        P(),
        P(),
        P(frame, fsdp),
        P(fsdp, frame),
    )
    return jax.shard_map(
        shards,
        mesh=fine,
        in_specs=placed,
        out_specs=P(frame, fsdp, None, None),
        check_vma=False,
    )
```

```python
import math

import jax
import jax.numpy as jnp
from jax import lax
from jax.experimental import pallas as pl
from jax.experimental.pallas import tpu as pltpu
from jax.sharding import Mesh
from jax.sharding import PartitionSpec as P

HEAD = 128
MESH = pl.DeviceIdType.MESH
BF = jnp.bfloat16
F32 = jnp.float32
AXES = ("zlo", "x", "core", "y", "zhi")
ANY = pl.BlockSpec(memory_space=pl.ANY)
VMEM = pl.BlockSpec(memory_space=pltpu.VMEM)
SMEM = pl.BlockSpec(memory_space=pltpu.SMEM)
SCALE2 = math.log2(math.e) / math.sqrt(HEAD)


def aligned(index, size):
    return pl.ds(pl.multiple_of(index * size, size), size)


class Place:
    def __init__(self):
        self.zlo, self.x, self.core, self.y, self.zhi = (lax.axis_index(a) for a in AXES)
        turn = 1 - 2 * self.core
        self.chip = self.zlo * 4 + self.x
        self.share = 2 * self.y + self.zhi
        self.xf, self.xb, self.xo = (lax.rem(self.x + 4 + k, 4) for k in (turn, -turn, 2))
        self.yf, self.yb, self.yo = (lax.rem(self.y + 4 + k, 4) for k in (turn, -turn, 2))
        self.partner = {"core": 1 - self.core}
        self.side = self.x // 2
        self.xs = self.x + 1 - 2 * lax.rem(self.x, 2)
        self.xp = 3 - self.x
        self.zq = self.zlo + 1 - 2 * lax.rem(self.zlo, 2)
        self.zi = 3 - self.zlo
        self.inner = jnp.logical_or(self.zlo == 1, self.zlo == 2)
        self.zsrc = [self.zlo, self.zq, 2 - self.zlo // 2, 3 - 3 * (self.zlo // 2)]
        self.far = {"zhi": 1 - self.zhi}


class Copies:
    def __init__(self, send, recv, local):
        self.send, self.recv, self.local = send, recv, local
        self.pushed, self.kept, self.count = {}, 0, 0

    def reserve(self):
        self.count += 1
        return self.count - 1

    def push(self, src, dst, device, lands=None, when=None):
        index = self.reserve()
        arrives = self.recv.at[index if lands is None else lands]
        copy = pltpu.make_async_remote_copy(
            src, dst, self.send.at[index], arrives, device_id=device, device_id_type=MESH
        )
        if when is None:
            copy.start()
        else:
            pl.when(when)(copy.start)
        self.pushed[index] = (copy, when)
        return index

    def hand(self, src, dst, device, here, lands):
        copy = pltpu.make_async_copy(src, dst, self.recv.at[lands])
        pl.when(here)(copy.start)
        self.push(src, dst, device, lands, jnp.logical_not(here))

    def got(self, index, region):
        pltpu.make_async_copy(region, region, self.recv.at[index]).wait()

    def keep(self, src, dst):
        copy = pltpu.make_async_copy(src, dst, self.local.at[self.kept])
        copy.start()
        self.kept += 1
        return copy

    def left(self, index):
        copy, when = self.pushed.pop(index)
        if when is None:
            copy.wait_send()
        else:
            pl.when(when)(copy.wait_send)

    def sent(self):
        for index in list(self.pushed):
            self.left(index)


class Line:
    def __init__(self, copies, at, region, x):
        self.copies, self.at, self.region, self.x = copies, at, region, x
        self.lands = [copies.reserve() for _ in range(3)]

    def block(self, k):
        return self.region(self.at.zsrc[k] * 4 + self.x)

    def start(self):
        block = self.block(0)
        self.copies.push(block, block, {"zlo": self.at.zq}, self.lands[0])
        self.copies.push(block, block, {"zlo": self.at.zi}, self.lands[1], self.at.inner)

    def arrive(self, k):
        block = self.block(k)
        self.copies.got(self.lands[k - 1], block)
        if k == 1:
            self.copies.push(block, block, {"zlo": self.at.zi}, self.lands[2], self.at.inner)
        else:
            self.copies.push(block, block, {"zlo": self.at.zq}, self.lands[k - 1], self.at.inner)


def greet(devices):
    barrier = pltpu.get_barrier_semaphore()
    for device in devices:
        pl.semaphore_signal(barrier, inc=1, device_id=device, device_id_type=MESH)
    pl.semaphore_wait(barrier, len(devices))


def x_start(copies, at, region, z):
    mine = region(z * 4 + at.x)
    return (
        copies.push(mine, mine, {"x": at.xf}),
        copies.push(mine, mine, {"x": at.xb}),
    )


def x_forward(copies, at, region, z, started):
    block = region(z * 4 + at.xb)
    copies.got(started[0], block)
    return copies.push(block, block, {"x": at.xf})


def x_rest(copies, at, region, z, started, forwarded):
    copies.got(started[1], region(z * 4 + at.xf))
    copies.got(forwarded, region(z * 4 + at.xo))


def scratch(pushes, locals_):
    return [
        pltpu.SemaphoreType.DMA((pushes,)),
        pltpu.SemaphoreType.DMA((pushes,)),
        pltpu.SemaphoreType.DMA((locals_,)),
    ]


def layer_kernel(
    times,
    tokens,
    wq,
    wo,
    up,
    down,
    gain,
    conv,
    out,
    tok,
    wq_here,
    stage,
    queries,
    kv,
    top,
    total,
    mixed,
    attn,
    wo_here,
    rows,
    residual,
    window,
    gathered,
    ud,
    hidden,
    terms,
    relay,
    direct,
    summed,
    final,
    send,
    recv,
    local,
):
    at = Place()
    copies = Copies(send, recv, local)
    width = out.shape[1]
    deep = at.zhi * 4 + at.zlo
    z_steps = (1, 7, 2, 6, 3, 5, 4)
    deep_to = [lax.rem(deep + k, 8) for k in z_steps]
    order = [deep] + [lax.rem(deep + 8 - k, 8) for k in z_steps]
    zsrc = at.zsrc
    peers = [(c, z, y) for z in (1, 0) for y in range(4) for c in (0, 1) if (c, z, y) != (0, 0, 0)]
    halves = (0, 1)

    def peer(c, z, y, sign):
        return (
            lax.rem(at.core + c, 2),
            lax.rem(at.zhi + z, 2),
            lax.rem(at.y + 4 + sign * y, 4),
        )

    def named(place):
        return {"core": place[0], "zhi": place[1], "y": place[2]}

    def depth(z):
        return {"zhi": z // 4, "zlo": lax.rem(z, 4)}

    greet(
        [named(peer(*p, 1)) for p in peers]
        + [{"x": at.xp, **named(peer(*p, 1))} for p in peers + [(0, 0, 0)]]
        + [{"x": at.xs}]
        + [depth(z) for z in deep_to[:-1]]
    )


    def piece(share, half):
        return tok.at[at.core, pl.ds(pl.multiple_of(share * 64 + half * 32, 32), 32)]

    def share_block(core, share):
        return tok.at[core, aligned(share, 64)]

    def wq_block(chip):
        return wq_here.at[aligned(chip, 192)]

    def wo_block(chip):
        return wo_here.at[pl.ds(2 * at.y, 2), chip, at.core]

    def wo_plane(y, core, k):
        return wo_here.at[pl.ds(2 * y, 2), aligned(zsrc[k], 4), core]

    def kv_block(chip):
        return kv.at[chip]

    source = [tokens.at[pl.ds(32 * h, 32)] for h in halves]

    def wq_piece(core, i):
        return wq_here.at[aligned(2 * at.chip + core, 96), pl.ds(HEAD * i, HEAD)]

    far = []
    w_pair = [
        copies.push(
            wq.at[i, :, aligned(1 - at.core, HEAD)], wq_piece(at.core, i), at.partner
        )
        for i in range(3)
    ]
    w_own = [
        copies.keep(wq.at[i, :, aligned(at.core, HEAD)], wq_piece(at.core, i)) for i in range(3)
    ]
    own_f = [copies.push(source[h], piece(at.share, h), {"y": at.yf}) for h in halves]
    own_b = [copies.push(source[h], piece(at.share, h), {"y": at.yb}) for h in halves]
    t_own = copies.keep(tokens, share_block(at.core, at.share))
    o_own = copies.keep(wo, wo_here.at[at.share, at.chip, at.core])
    own_ud = [
        copies.keep(ref, ud.at[i, at.chip, at.core, :, aligned(at.zhi, 384)])
        for i, ref in enumerate((up, down))
    ]
    shared = []

    def share_out(share):
        block = share_block(at.core, share)
        shared.append((copies.push(block, block, at.partner), share))

    for i in range(3):
        w_own[i].wait()
        copies.got(w_pair[i], wq_piece(1 - at.core, i))
    w_line = Line(copies, at, wq_block, at.x)
    w_line.start()
    w_x = [x_start(copies, at, wq_block, at.zlo)]
    far.append(copies.push(source[0], piece(at.share, 0), at.far))
    far.append(copies.push(source[1], piece(at.share, 1), at.far))
    o_far = copies.push(wo, wo_here.at[at.share, at.chip, at.core], at.far)
    t_own.wait()
    share_out(at.share)
    far_share = 2 * at.y + 1 - at.zhi
    near_ring = [2 * y + at.zhi for y in (at.yb, at.yf, at.yo)]
    far_ring = [2 * y + 1 - at.zhi for y in (at.yb, at.yf, at.yo)]
    fwd, far_f, far_b = [], [], []

    def pass_tokens(index, share, half):
        block = piece(share, half)
        copies.got(index, block)
        return copies.push(block, block, {"y": at.yf})

    def spread_far(h):
        block = piece(far_share, h)
        copies.got(far[h], block)
        far_f.append(copies.push(block, block, {"y": at.yf}))
        far_b.append(copies.push(block, block, {"y": at.yb}))

    w_f = []

    def w_open(k):
        w_line.arrive(k)
        w_x.append(x_start(copies, at, wq_block, zsrc[k]))

    def w_forward(k):
        w_f.append(x_forward(copies, at, wq_block, zsrc[k], w_x[k]))

    fwd.append(pass_tokens(own_f[0], near_ring[0], 0))
    w_forward(0)
    w_open(1)
    fwd.append(pass_tokens(own_f[1], near_ring[0], 1))
    share_out(near_ring[0])
    w_forward(1)
    w_open(2)
    for h in halves:
        copies.got(own_b[h], piece(near_ring[1], h))
    share_out(near_ring[1])
    w_open(3)
    w_forward(2)
    spread_far(0)
    for h in halves:
        copies.got(fwd[h], piece(near_ring[2], h))
    share_out(near_ring[2])
    w_forward(3)
    spread_far(1)
    share_out(far_share)
    o_own.wait()
    copies.got(o_far, wo_here.at[far_share, at.chip, at.core])
    o_line = Line(copies, at, wo_block, at.x)
    o_line.start()
    o_x, o_f = [x_start(copies, at, wo_block, at.zlo)], []

    def o_open(k):
        o_line.arrive(k)
        o_x.append(x_start(copies, at, wo_block, zsrc[k]))

    def o_forward(k):
        o_f.append(x_forward(copies, at, wo_block, zsrc[k], o_x[k]))

    o_y, o_fwd, o_over = {}, {}, {}

    def o_spread(k):
        x_rest(copies, at, wo_block, zsrc[k], o_x[k], o_f[k])
        plane = wo_plane(at.y, at.core, k)
        o_y[k] = [copies.push(plane, plane, {"y": y}) for y in (at.yf, at.yb)]
        o_over[k] = [copies.push(plane, plane, at.partner)]

    def o_relay(k):
        plane = wo_plane(at.yb, at.core, k)
        copies.got(o_y[k][0], plane)
        o_fwd[k] = copies.push(plane, plane, {"y": at.yf})
        o_over[k].append(copies.push(plane, plane, at.partner))
        plane = wo_plane(at.yf, at.core, k)
        copies.got(o_y[k][1], plane)
        o_over[k].append(copies.push(plane, plane, at.partner))

    def o_last(k):
        plane = wo_plane(at.yo, at.core, k)
        copies.got(o_fwd[k], plane)
        o_over[k].append(copies.push(plane, plane, at.partner))

    fwd = []
    for h in halves:
        fwd.append(pass_tokens(far_f[h], far_ring[0], h))
    share_out(far_ring[0])
    o_open(1)
    for h in halves:
        copies.got(far_b[h], piece(far_ring[1], h))
    share_out(far_ring[1])
    o_forward(0)
    o_open(2)
    for h in halves:
        copies.got(fwd[h], piece(far_ring[2], h))
    share_out(far_ring[2])
    o_open(3)
    for k in range(4):
        x_rest(copies, at, wq_block, zsrc[k], w_x[k], w_f[k])
    o_spread(0)
    for index, share in shared:
        copies.got(index, share_block(1 - at.core, share))


    native = at.core == at.side
    across = {"x": at.xp, "core": 1 - at.core}
    px = at.core * at.side + (1 - at.core) * (1 - at.side)
    px = px * at.x + (1 - px) * at.xp
    pxs = px + 1 - 2 * lax.rem(px, 2)
    held = at.zlo * 4 + px
    handed = [copies.reserve() for _ in range(3)]
    for t in range(2):
        part = pl.ds(512 * t, 512)
        both = jnp.dot(tok[t], wq_here[:, HEAD:], preferred_element_type=F32).astype(BF)
        stage[1, part, :] = both[:, :HEAD]
        stage[2, part, :] = both[:, HEAD:]
        copies.hand(
            stage.at[pl.ds(1, 2), part], kv.at[at.chip, :, part], across, native, handed[t]
        )
    for t in range(2):
        stage[0, pl.ds(512 * t, 512), :] = jnp.dot(
            tok[t], wq_here[:, :HEAD], preferred_element_type=F32
        ).astype(BF)
    copies.hand(stage.at[0], queries, across, native, handed[2])
    top[...] = jnp.full_like(top, -1e30)
    total[...] = jnp.zeros_like(total)
    mixed[...] = jnp.zeros_like(mixed)
    for t in range(2):
        copies.got(handed[t], kv.at[held, :, pl.ds(512 * t, 512)])

    def attend(chip):
        for t in range(2):
            part_rows = slice(512 * t, 512 * t + 512)
            own_time = times[2 * held + t]
            scores = lax.dot_general(
                queries[part_rows, :],
                kv[chip, 0],
                (((1,), (1,)), ((), ())),
                preferred_element_type=F32,
            )
            seen = [times[2 * chip + j] <= own_time for j in (0, 1)]
            parts = [scores[:, :512], scores[:, 512:]]
            old = top[part_rows, :1]
            new = old
            for part, see in zip(parts, seen):
                new = jnp.maximum(
                    new, jnp.where(see, jnp.max(part, axis=1, keepdims=True), -1e30)
                )
            decay = jnp.exp2((old - new) * SCALE2)
            weights = [
                jnp.exp2((part - jnp.where(see, new, 1e30)) * SCALE2)
                for part, see in zip(parts, seen)
            ]
            lanes = total[part_rows, :] * decay
            for part in weights:
                for j in range(4):
                    lanes = lanes + part[:, 128 * j : 128 * j + 128]
            total[part_rows, :] = lanes
            top[part_rows, :] = jnp.broadcast_to(new, (512, 128))
            both = jnp.concatenate([part.astype(BF) for part in weights], axis=1)
            mixed[part_rows, :] = mixed[part_rows, :] * decay + jnp.dot(
                both, kv[chip, 1], preferred_element_type=F32
            )

    kv_line = Line(copies, at, kv_block, px)
    beside, columns_over, beside_over = [], [], []

    def column(k, x):
        return kv_block(zsrc[k] * 4 + x)

    def kv_open(k):
        block = column(k, px)
        if k == 0:
            kv_line.start()
        else:
            kv_line.arrive(k)
        beside.append(copies.push(block, block, {"x": at.xs}))
        columns_over.append(copies.push(block, block, at.partner))

    def kv_beside(k):
        block = column(k, pxs)
        copies.got(beside[k], block)
        beside_over.append(copies.push(block, block, at.partner))

    def attend_column(k):
        attend(zsrc[k] * 4 + px)

    def attend_beside(k):
        attend(zsrc[k] * 4 + pxs)

    def attend_column_over(k):
        copies.got(columns_over[k], column(k, 3 - px))
        attend(zsrc[k] * 4 + 3 - px)

    def attend_beside_over(k):
        copies.got(beside_over[k], column(k, 3 - pxs))
        attend(zsrc[k] * 4 + 3 - pxs)

    def ud_block(z, x):
        return ud.at[:, lax.rem(z, 4) * 4 + x, at.core, :, aligned(z // 4, 384)]

    def ud_lump(z, core):
        return ud.at[:, aligned(lax.rem(z, 4), 4), core, :, aligned(z // 4, 384)]

    def x_push(z):
        block = ud_block(z, at.x)
        return (copies.push(block, block, {"x": at.xf}), copies.push(block, block, {"x": at.xb}))

    kv_open(0)
    for k in (1, 2, 3):
        o_forward(k)
    copies.got(handed[2], queries)
    attend_column(0)
    for k in (1, 2, 3):
        o_spread(k)
    attend_column_over(0)
    o_relay(0)
    kv_open(1)
    kv_beside(0)
    attend_beside(0)
    attend_column(1)
    o_last(0)
    attend_column_over(1)
    attend_beside_over(0)
    kv_open(2)
    kv_beside(1)
    o_relay(1)
    attend_beside(1)
    attend_column(2)
    attend_column_over(2)
    attend_beside_over(1)
    kv_open(3)
    for copy in own_ud:
        copy.wait()
    block = ud_block(deep, at.x)
    along_z = [copies.push(block, block, depth(z)) for z in deep_to]
    kv_beside(2)
    o_relay(2)
    o_last(1)
    attend_beside(2)
    attend_column(3)
    attend_column_over(3)
    attend_beside_over(2)
    kv_beside(3)
    opened, forwarded, lumps = [x_push(deep)], [], []

    def open_group(k):
        copies.got(along_z[k - 1], ud_block(order[k], at.x))
        opened.append(x_push(order[k]))

    o_relay(3)
    o_last(2)
    attend_beside(3)
    for k in (1, 2):
        open_group(k)
    attend_beside_over(3)
    for t in range(2):
        part_rows = slice(512 * t, 512 * t + 512)
        attn[t] = (
            mixed[part_rows, :] / jnp.sum(total[part_rows, :], axis=1, keepdims=True)
        ).astype(BF)


    def head_rows(head):
        return rows.at[:, aligned(head, HEAD)]

    def first_row(share):
        return jnp.clip(2 * share - 1, 0, 12)

    def needed(place):
        core, zhi, y = place
        return attn.at[core, pl.ds(pl.multiple_of(first_row(2 * y + zhi) * 32, 32), 128)]

    head = 2 * at.share + at.side
    first = first_row(at.share)
    role = at.core + at.side - 2 * at.core * at.side
    places = [(z, y) for z in (1, 0) for y in range(4)]
    arrivals = []
    for z, y in places:
        base = copies.reserve()
        copies.reserve()
        arrivals.append(base)
        for c in (0, 1):
            _, zhi, y_to = peer(0, z, y, 1)
            goal = (lax.rem(at.core + c, 2), zhi, y_to)
            device = {"x": px, **named(goal)}
            if (c, z, y) == (0, 0, 0):
                copies.hand(needed(goal), head_rows(head), device, native, base + role)
            else:
                copies.push(needed(goal), head_rows(head), device, base + role)
    def forward_group(k):
        block = ud_block(order[k], at.xb)
        copies.got(opened[k][0], block)
        forwarded.append(copies.push(block, block, {"x": at.xf}))

    def close_group(k):
        copies.got(opened[k][1], ud_block(order[k], at.xf))
        copies.got(forwarded[k], ud_block(order[k], at.xo))
        lump = ud_lump(order[k], at.core)
        lumps.append(copies.push(lump, lump, at.partner))

    shift = 2 * at.share - 1 - first
    for r in (1, 4):
        window[r] = jnp.zeros(window.shape[1:], F32)
    open_group(3)
    forward_group(0)
    o_last(3)
    for base, (z, y) in zip(arrivals, places):
        _, zhi, y_from = peer(0, z, y, -1)
        whose = 2 * (2 * y_from + zhi)
        copies.got(base, head_rows(whose + at.side))
        copies.got(base + 1, head_rows(whose + 1 - at.side))
    for k in range(4):
        for index, y in zip(o_over[k], (at.y, at.yb, at.yf, at.yo)):
            copies.got(index, wo_plane(y, 1 - at.core, k))
    for k in (4, 5):
        open_group(k)
    forward_group(1)
    near_rows = pl.ds(pl.multiple_of(first * 32, 32), 128)

    def project(n, carry):
        columns = aligned(n, 768)
        acc = tok[at.core, near_rows, columns].astype(F32)
        for s in range(8):
            acc = acc + lax.dot_general(
                rows[:, 256 * s : 256 * s + 256],
                wo_here[s, pl.ds(4 * n, 4)].reshape(768, 256),
                (((1,), (1,)), ((), ())),
                preferred_element_type=F32,
            )
        residual[:, columns] = acc
        return carry

    lax.fori_loop(0, 4, project, 0)
    for k in (6, 7):
        open_group(k)
    forward_group(2)
    close_group(0)
    forward_group(3)
    for r in range(4):
        row = residual[32 * r : 32 * r + 32, :]
        mean_square = jnp.mean(row * row, axis=1, keepdims=True)
        normed = row * lax.rsqrt(mean_square + 1e-06) * gain[...].astype(F32)
        window[1 + r - shift] = normed.astype(BF).astype(F32)
    close_group(1)
    line = lax.broadcasted_iota(jnp.int32, (32, 512), 0)

    def convolve(j):
        def tile(n, carry):
            columns = aligned(n, 512)
            sums = [jnp.zeros((32, 512), F32)] * 3
            for a in range(3):
                taps = conv[a, :, columns].astype(F32)
                values = window[1 + j + a, :, columns]
                for b in range(3):
                    sums[b] = sums[b] + values * taps[b : b + 1, :]
            before = jnp.where(line == 0, 0.0, pltpu.roll(sums[0], 1, 0))
            after = jnp.where(line == 31, 0.0, pltpu.roll(sums[2], 31, 0))
            gathered[aligned(2 * at.y + j, 32), columns] = (before + sums[1] + after).astype(BF)
            return carry

        lax.fori_loop(0, width // 512, tile, 0)

    def token_piece(y, h):
        return gathered.at[aligned(2 * y + h, 32)]

    ahead, behind = [], []
    for h in (0, 1):
        convolve(h)
        piece = token_piece(at.y, h)
        ahead.append(copies.push(piece, piece, {"y": at.yf}))
        behind.append(copies.push(piece, piece, {"y": at.yb}))
    forward_group(4)
    close_group(2)
    token_fwd = []
    for h in (0, 1):
        piece = token_piece(at.yb, h)
        copies.got(ahead[h], piece)
        token_fwd.append(copies.push(piece, piece, {"y": at.yf}))
    close_group(3)
    for k in (5, 6, 7):
        forward_group(k)
        close_group(k - 1)
    close_group(7)
    for h in (0, 1):
        copies.got(behind[h], token_piece(at.yf, h))
        copies.got(token_fwd[h], token_piece(at.yo, h))
    for index, z in zip(lumps, order):
        copies.got(index, ud_lump(z, 1 - at.core))

    for n in range(3):
        columns = slice(256 * n, 256 * n + 256)
        value = jnp.dot(
            gathered[...],
            ud[0, :, :, :, columns].reshape(width, 256),
            preferred_element_type=F32,
        )
        hidden[:, columns] = jax.nn.gelu(value).astype(BF)

    chunk = width // 4

    def columns_of(q):
        return slice(chunk * q, chunk * q + chunk)

    def term(y, q):
        return terms.at[aligned(y, 64), pl.ds(chunk * q, chunk)]

    def strip(ref, q):
        return ref.at[:, pl.ds(chunk * q, chunk)]

    relays, directs, finals = [], [], []

    def pass_on(q):
        copies.got(relays[q], strip(relay, q))
        columns = columns_of(q)
        summed[:, columns] = (
            terms[aligned(at.yf, 64), columns].astype(F32) + relay[:, columns].astype(F32)
        ).astype(BF)
        finals.append(copies.push(strip(summed, q), strip(final, q), {"y": at.yf}))

    for q in range(4):
        terms[:, columns_of(q)] = lax.dot_general(
            hidden[...],
            ud[1, 4 * q : 4 * q + 4].reshape(chunk, chunk),
            (((1,), (1,)), ((), ())),
            preferred_element_type=F32,
        ).astype(BF)
        relays.append(copies.push(term(at.yo, q), strip(relay, q), {"y": at.yf}))
        directs.append(copies.push(term(at.yb, q), strip(direct, q), {"y": at.yb}))
        if q > 0:
            pass_on(q - 1)
    pass_on(3)
    own_rows = pl.ds(pl.multiple_of((1 + shift) * 32, 32), 64)
    for q in range(4):
        columns = columns_of(q)
        copies.got(directs[q], strip(direct, q))
        partial = (
            residual[own_rows, columns]
            + terms[aligned(at.y, 64), columns].astype(F32)
            + direct[:, columns].astype(F32)
        )
        copies.got(finals[q], strip(final, q))
        out[:, columns] = (partial + final[:, columns].astype(F32)).astype(BF)
    copies.sent()


def remote(collective_id, megabytes=32):
    return pltpu.CompilerParams(
        collective_id=collective_id, has_side_effects=True, vmem_limit_bytes=megabytes << 20
    )


def shape(*dims, dtype=BF):
    return jax.ShapeDtypeStruct(dims, dtype)


def shards(
    tokens, frame_time, qkv_weight, out_weight, norm_gain, conv_weight, up_weight, down_weight
):
    width = tokens.shape[3]
    result = pl.pallas_call(
        layer_kernel,
        out_shape=shape(64, width),
        in_specs=[SMEM] + [ANY] * 5 + [VMEM] * 2,
        out_specs=VMEM,
        scratch_shapes=[
            pltpu.VMEM((2, 512, width), BF),
            pltpu.VMEM((width, 3 * HEAD), BF),
            pltpu.VMEM((3, 1024, HEAD), BF),
            pltpu.VMEM((1024, HEAD), BF),
            pltpu.VMEM((16, 2, 1024, HEAD), BF),
            pltpu.VMEM((1024, HEAD), F32),
            pltpu.VMEM((1024, HEAD), F32),
            pltpu.VMEM((1024, HEAD), F32),
            pltpu.VMEM((2, 512, HEAD), BF),
            pltpu.VMEM((8, 16, 2, 96, 256), BF),
            pltpu.VMEM((128, 16 * HEAD), BF),
            pltpu.VMEM((128, width), F32),
            pltpu.VMEM((6, 32, width), F32),
            pltpu.VMEM((256, width), BF),
            pltpu.VMEM((2, 16, 2, 96, 768), BF),
            pltpu.VMEM((256, 768), BF),
            pltpu.VMEM((256, width), BF),
        ]
        + [pltpu.VMEM((64, width), BF)] * 4
        + scratch(288, 8),
        compiler_params=remote(1, 60),
    )(
        frame_time,
        tokens.reshape(64, width),
        qkv_weight,
        out_weight.T,
        up_weight,
        down_weight.T,
        norm_gain.reshape(1, width),
        conv_weight,
    )
    return result.reshape(1, 2, 32, width)


def solution(mesh):
    fine = Mesh(mesh.devices.reshape(4, 4, 2, 4, 2), AXES)
    frame, fsdp = ("zlo", "x", "core"), ("y", "zhi")
    placed = (
        P(frame, fsdp, None, None),
        P(),
        P(None, frame, fsdp),
        P(fsdp, frame),
        P(),
        P(),
        P(frame, fsdp),
        P(fsdp, frame),
    )
    return jax.shard_map(
        shards,
        mesh=fine,
        in_specs=placed,
        out_specs=P(frame, fsdp, None, None),
        check_vma=False,
    )
```

```python
import math

import jax
import jax.numpy as jnp
from jax import lax
from jax.experimental import pallas as pl
from jax.experimental.pallas import tpu as pltpu
from jax.sharding import Mesh
from jax.sharding import PartitionSpec as P

HEAD = 128
MESH = pl.DeviceIdType.MESH
BF = jnp.bfloat16
F32 = jnp.float32
AXES = ("zlo", "x", "core", "y", "zhi")
ANY = pl.BlockSpec(memory_space=pl.ANY)
VMEM = pl.BlockSpec(memory_space=pltpu.VMEM)
SMEM = pl.BlockSpec(memory_space=pltpu.SMEM)
SCALE2 = math.log2(math.e) / math.sqrt(HEAD)


def aligned(index, size):
    return pl.ds(pl.multiple_of(index * size, size), size)


class Place:
    def __init__(self):
        self.zlo, self.x, self.core, self.y, self.zhi = (lax.axis_index(a) for a in AXES)
        turn = 1 - 2 * self.core
        self.chip = self.zlo * 4 + self.x
        self.share = 2 * self.y + self.zhi
        self.xf, self.xb, self.xo = (lax.rem(self.x + 4 + k, 4) for k in (turn, -turn, 2))
        self.yf, self.yb, self.yo = (lax.rem(self.y + 4 + k, 4) for k in (turn, -turn, 2))
        self.partner = {"core": 1 - self.core}
        self.side = self.x // 2
        self.xs = self.x + 1 - 2 * lax.rem(self.x, 2)
        self.xp = 3 - self.x
        self.zq = self.zlo + 1 - 2 * lax.rem(self.zlo, 2)
        self.zi = 3 - self.zlo
        self.inner = jnp.logical_or(self.zlo == 1, self.zlo == 2)
        self.zsrc = [self.zlo, self.zq, 2 - self.zlo // 2, 3 - 3 * (self.zlo // 2)]
        self.far = {"zhi": 1 - self.zhi}


class Copies:
    def __init__(self, send, recv, local):
        self.send, self.recv, self.local = send, recv, local
        self.pushed, self.kept, self.count = {}, 0, 0

    def reserve(self):
        self.count += 1
        return self.count - 1

    def push(self, src, dst, device, lands=None, when=None):
        index = self.reserve()
        arrives = self.recv.at[index if lands is None else lands]
        copy = pltpu.make_async_remote_copy(
            src, dst, self.send.at[index], arrives, device_id=device, device_id_type=MESH
        )
        if when is None:
            copy.start()
        else:
            pl.when(when)(copy.start)
        self.pushed[index] = (copy, when)
        return index

    def hand(self, src, dst, device, here, lands):
        copy = pltpu.make_async_copy(src, dst, self.recv.at[lands])
        pl.when(here)(copy.start)
        self.push(src, dst, device, lands, jnp.logical_not(here))

    def got(self, index, region):
        pltpu.make_async_copy(region, region, self.recv.at[index]).wait()

    def keep(self, src, dst):
        copy = pltpu.make_async_copy(src, dst, self.local.at[self.kept])
        copy.start()
        self.kept += 1
        return copy

    def left(self, index):
        copy, when = self.pushed.pop(index)
        if when is None:
            copy.wait_send()
        else:
            pl.when(when)(copy.wait_send)

    def sent(self):
        for index in list(self.pushed):
            self.left(index)


class Line:
    def __init__(self, copies, at, region, x):
        self.copies, self.at, self.region, self.x = copies, at, region, x
        self.lands = [copies.reserve() for _ in range(3)]

    def block(self, k):
        return self.region(self.at.zsrc[k] * 4 + self.x)

    def start(self):
        block = self.block(0)
        self.copies.push(block, block, {"zlo": self.at.zq}, self.lands[0])
        self.copies.push(block, block, {"zlo": self.at.zi}, self.lands[1], self.at.inner)

    def arrive(self, k):
        block = self.block(k)
        self.copies.got(self.lands[k - 1], block)
        if k == 1:
            self.copies.push(block, block, {"zlo": self.at.zi}, self.lands[2], self.at.inner)
        else:
            self.copies.push(block, block, {"zlo": self.at.zq}, self.lands[k - 1], self.at.inner)


def greet(devices):
    barrier = pltpu.get_barrier_semaphore()
    for device in devices:
        pl.semaphore_signal(barrier, inc=1, device_id=device, device_id_type=MESH)
    pl.semaphore_wait(barrier, len(devices))


def x_start(copies, at, region, z):
    mine = region(z * 4 + at.x)
    return (
        copies.push(mine, mine, {"x": at.xf}),
        copies.push(mine, mine, {"x": at.xb}),
    )


def x_forward(copies, at, region, z, started):
    block = region(z * 4 + at.xb)
    copies.got(started[0], block)
    return copies.push(block, block, {"x": at.xf})


def x_rest(copies, at, region, z, started, forwarded):
    copies.got(started[1], region(z * 4 + at.xf))
    copies.got(forwarded, region(z * 4 + at.xo))


def scratch(pushes, locals_):
    return [
        pltpu.SemaphoreType.DMA((pushes,)),
        pltpu.SemaphoreType.DMA((pushes,)),
        pltpu.SemaphoreType.DMA((locals_,)),
    ]


def layer_kernel(
    times,
    tokens,
    wq,
    wo,
    up,
    down,
    gain,
    conv,
    out,
    tok,
    wq_here,
    stage,
    queries,
    kv,
    top,
    total,
    mixed,
    attn,
    wo_here,
    rows,
    residual,
    window,
    gathered,
    ud,
    hidden,
    terms,
    relay,
    direct,
    summed,
    final,
    send,
    recv,
    local,
):
    at = Place()
    copies = Copies(send, recv, local)
    width = out.shape[1]
    deep = at.zhi * 4 + at.zlo
    z_steps = (1, 7, 2, 6, 3, 5, 4)
    deep_to = [lax.rem(deep + k, 8) for k in z_steps]
    order = [deep] + [lax.rem(deep + 8 - k, 8) for k in z_steps]
    zsrc = at.zsrc
    peers = [(c, z, y) for z in (1, 0) for y in range(4) for c in (0, 1) if (c, z, y) != (0, 0, 0)]
    halves = (0, 1)

    def peer(c, z, y, sign):
        return (
            lax.rem(at.core + c, 2),
            lax.rem(at.zhi + z, 2),
            lax.rem(at.y + 4 + sign * y, 4),
        )

    def named(place):
        return {"core": place[0], "zhi": place[1], "y": place[2]}

    def depth(z):
        return {"zhi": z // 4, "zlo": lax.rem(z, 4)}

    greet(
        [named(peer(*p, 1)) for p in peers]
        + [{"x": at.xp, **named(peer(*p, 1))} for p in peers + [(0, 0, 0)]]
        + [{"x": at.xs}]
        + [depth(z) for z in deep_to[:-1]]
    )


    def piece(share, half):
        return tok.at[at.core, pl.ds(pl.multiple_of(share * 64 + half * 32, 32), 32)]

    def share_block(core, share):
        return tok.at[core, aligned(share, 64)]

    def wq_block(chip):
        return wq_here.at[aligned(chip, 192)]

    def wo_block(chip):
        return wo_here.at[pl.ds(2 * at.y, 2), chip, at.core]

    def wo_plane(y, core, k):
        return wo_here.at[pl.ds(2 * y, 2), aligned(zsrc[k], 4), core]

    def kv_block(chip):
        return kv.at[chip]

    source = [tokens.at[pl.ds(32 * h, 32)] for h in halves]

    def wq_piece(core, i):
        return wq_here.at[aligned(2 * at.chip + core, 96), pl.ds(HEAD * i, HEAD)]

    far = []
    w_pair = [
        copies.push(
            wq.at[i, :, aligned(1 - at.core, HEAD)], wq_piece(at.core, i), at.partner
        )
        for i in range(3)
    ]
    w_own = [
        copies.keep(wq.at[i, :, aligned(at.core, HEAD)], wq_piece(at.core, i)) for i in range(3)
    ]
    own_f = [copies.push(source[h], piece(at.share, h), {"y": at.yf}) for h in halves]
    own_b = [copies.push(source[h], piece(at.share, h), {"y": at.yb}) for h in halves]
    t_own = copies.keep(tokens, share_block(at.core, at.share))
    o_own = copies.keep(wo, wo_here.at[at.share, at.chip, at.core])
    own_ud = [
        copies.keep(ref, ud.at[i, at.chip, at.core, :, aligned(at.zhi, 384)])
        for i, ref in enumerate((up, down))
    ]
    shared = []

    def share_out(share):
        block = share_block(at.core, share)
        shared.append((copies.push(block, block, at.partner), share))

    for i in range(3):
        w_own[i].wait()
        copies.got(w_pair[i], wq_piece(1 - at.core, i))
    w_line = Line(copies, at, wq_block, at.x)
    w_line.start()
    w_x = [x_start(copies, at, wq_block, at.zlo)]
    far.append(copies.push(source[0], piece(at.share, 0), at.far))
    far.append(copies.push(source[1], piece(at.share, 1), at.far))
    o_far = copies.push(wo, wo_here.at[at.share, at.chip, at.core], at.far)
    t_own.wait()
    share_out(at.share)
    far_share = 2 * at.y + 1 - at.zhi
    near_ring = [2 * y + at.zhi for y in (at.yb, at.yf, at.yo)]
    far_ring = [2 * y + 1 - at.zhi for y in (at.yb, at.yf, at.yo)]
    fwd, far_f, far_b = [], [], []

    def pass_tokens(index, share, half):
        block = piece(share, half)
        copies.got(index, block)
        return copies.push(block, block, {"y": at.yf})

    def spread_far(h):
        block = piece(far_share, h)
        copies.got(far[h], block)
        far_f.append(copies.push(block, block, {"y": at.yf}))
        far_b.append(copies.push(block, block, {"y": at.yb}))

    w_f = []

    def w_open(k):
        w_line.arrive(k)
        w_x.append(x_start(copies, at, wq_block, zsrc[k]))

    def w_forward(k):
        w_f.append(x_forward(copies, at, wq_block, zsrc[k], w_x[k]))

    fwd.append(pass_tokens(own_f[0], near_ring[0], 0))
    w_forward(0)
    w_open(1)
    fwd.append(pass_tokens(own_f[1], near_ring[0], 1))
    share_out(near_ring[0])
    w_forward(1)
    w_open(2)
    for h in halves:
        copies.got(own_b[h], piece(near_ring[1], h))
    share_out(near_ring[1])
    w_open(3)
    w_forward(2)
    spread_far(0)
    for h in halves:
        copies.got(fwd[h], piece(near_ring[2], h))
    share_out(near_ring[2])
    w_forward(3)
    spread_far(1)
    share_out(far_share)
    o_own.wait()
    copies.got(o_far, wo_here.at[far_share, at.chip, at.core])
    o_line = Line(copies, at, wo_block, at.x)
    o_line.start()
    o_x, o_f = [x_start(copies, at, wo_block, at.zlo)], []

    def o_open(k):
        o_line.arrive(k)
        o_x.append(x_start(copies, at, wo_block, zsrc[k]))

    def o_forward(k):
        o_f.append(x_forward(copies, at, wo_block, zsrc[k], o_x[k]))

    o_y, o_fwd, o_over = {}, {}, {}

    def o_spread(k):
        x_rest(copies, at, wo_block, zsrc[k], o_x[k], o_f[k])
        plane = wo_plane(at.y, at.core, k)
        o_y[k] = [copies.push(plane, plane, {"y": y}) for y in (at.yf, at.yb)]
        o_over[k] = [copies.push(plane, plane, at.partner)]

    def o_relay(k):
        plane = wo_plane(at.yb, at.core, k)
        copies.got(o_y[k][0], plane)
        o_fwd[k] = copies.push(plane, plane, {"y": at.yf})
        o_over[k].append(copies.push(plane, plane, at.partner))
        plane = wo_plane(at.yf, at.core, k)
        copies.got(o_y[k][1], plane)
        o_over[k].append(copies.push(plane, plane, at.partner))

    def o_last(k):
        plane = wo_plane(at.yo, at.core, k)
        copies.got(o_fwd[k], plane)
        o_over[k].append(copies.push(plane, plane, at.partner))

    fwd = []
    for h in halves:
        fwd.append(pass_tokens(far_f[h], far_ring[0], h))
    share_out(far_ring[0])
    o_open(1)
    for h in halves:
        copies.got(far_b[h], piece(far_ring[1], h))
    share_out(far_ring[1])
    o_forward(0)
    o_open(2)
    for h in halves:
        copies.got(fwd[h], piece(far_ring[2], h))
    share_out(far_ring[2])
    o_open(3)
    for k in range(4):
        x_rest(copies, at, wq_block, zsrc[k], w_x[k], w_f[k])
    o_spread(0)

    def ud_block(z, x):
        return ud.at[:, lax.rem(z, 4) * 4 + x, at.core, :, aligned(z // 4, 384)]

    def ud_lump(z, core):
        return ud.at[:, aligned(lax.rem(z, 4), 4), core, :, aligned(z // 4, 384)]

    def x_push(z):
        block = ud_block(z, at.x)
        return (copies.push(block, block, {"x": at.xf}), copies.push(block, block, {"x": at.xb}))

    for copy in own_ud:
        copy.wait()
    own_block = ud_block(deep, at.x)
    along_z, opened, forwarded, lumps = [], [], [], []

    def ud_along(first, last):
        for z in deep_to[first:last]:
            along_z.append(copies.push(own_block, own_block, depth(z)))

    def open_group(k):
        copies.got(along_z[k - 1], ud_block(order[k], at.x))
        opened.append(x_push(order[k]))

    ud_along(0, 4)
    for index, share in shared:
        copies.got(index, share_block(1 - at.core, share))


    native = at.core == at.side
    across = {"x": at.xp, "core": 1 - at.core}
    px = at.core * at.side + (1 - at.core) * (1 - at.side)
    px = px * at.x + (1 - px) * at.xp
    pxs = px + 1 - 2 * lax.rem(px, 2)
    held = at.zlo * 4 + px
    handed = [copies.reserve() for _ in range(3)]
    for t in range(2):
        part = pl.ds(512 * t, 512)
        both = jnp.dot(tok[t], wq_here[:, HEAD:], preferred_element_type=F32).astype(BF)
        stage[1, part, :] = both[:, :HEAD]
        stage[2, part, :] = both[:, HEAD:]
        copies.hand(
            stage.at[pl.ds(1, 2), part], kv.at[at.chip, :, part], across, native, handed[t]
        )
    for t in range(2):
        stage[0, pl.ds(512 * t, 512), :] = jnp.dot(
            tok[t], wq_here[:, :HEAD], preferred_element_type=F32
        ).astype(BF)
    copies.hand(stage.at[0], queries, across, native, handed[2])
    top[...] = jnp.full_like(top, -1e30)
    total[...] = jnp.zeros_like(total)
    mixed[...] = jnp.zeros_like(mixed)
    for t in range(2):
        copies.got(handed[t], kv.at[held, :, pl.ds(512 * t, 512)])

    def attend(chip):
        for t in range(2):
            part_rows = slice(512 * t, 512 * t + 512)
            own_time = times[2 * held + t]
            scores = lax.dot_general(
                queries[part_rows, :],
                kv[chip, 0],
                (((1,), (1,)), ((), ())),
                preferred_element_type=F32,
            )
            seen = [times[2 * chip + j] <= own_time for j in (0, 1)]
            parts = [scores[:, :512], scores[:, 512:]]
            old = top[part_rows, :1]
            new = old
            for part, see in zip(parts, seen):
                new = jnp.maximum(
                    new, jnp.where(see, jnp.max(part, axis=1, keepdims=True), -1e30)
                )
            decay = jnp.exp2((old - new) * SCALE2)
            weights = [
                jnp.exp2((part - jnp.where(see, new, 1e30)) * SCALE2)
                for part, see in zip(parts, seen)
            ]
            lanes = total[part_rows, :] * decay
            for part in weights:
                for j in range(4):
                    lanes = lanes + part[:, 128 * j : 128 * j + 128]
            total[part_rows, :] = lanes
            top[part_rows, :] = jnp.broadcast_to(new, (512, 128))
            both = jnp.concatenate([part.astype(BF) for part in weights], axis=1)
            mixed[part_rows, :] = mixed[part_rows, :] * decay + jnp.dot(
                both, kv[chip, 1], preferred_element_type=F32
            )

    kv_line = Line(copies, at, kv_block, px)
    beside, columns_over, beside_over = [], [], []

    def column(k, x):
        return kv_block(zsrc[k] * 4 + x)

    def kv_open(k):
        block = column(k, px)
        if k == 0:
            kv_line.start()
        else:
            kv_line.arrive(k)
        beside.append(copies.push(block, block, {"x": at.xs}))
        columns_over.append(copies.push(block, block, at.partner))

    def kv_beside(k):
        block = column(k, pxs)
        copies.got(beside[k], block)
        beside_over.append(copies.push(block, block, at.partner))

    def attend_column(k):
        attend(zsrc[k] * 4 + px)

    def attend_beside(k):
        attend(zsrc[k] * 4 + pxs)

    def attend_column_over(k):
        copies.got(columns_over[k], column(k, 3 - px))
        attend(zsrc[k] * 4 + 3 - px)

    def attend_beside_over(k):
        copies.got(beside_over[k], column(k, 3 - pxs))
        attend(zsrc[k] * 4 + 3 - pxs)

    kv_open(0)
    for k in (1, 2, 3):
        o_forward(k)
    copies.got(handed[2], queries)
    attend_column(0)
    attend_column_over(0)
    kv_open(1)
    kv_beside(0)
    attend_beside(0)
    for k in (1, 2, 3):
        o_spread(k)
    attend_column(1)
    attend_column_over(1)
    attend_beside_over(0)
    kv_open(2)
    kv_beside(1)
    attend_beside(1)
    attend_column(2)
    o_relay(0)
    attend_column_over(2)
    attend_beside_over(1)
    kv_open(3)
    ud_along(4, 7)
    kv_beside(2)
    attend_beside(2)
    attend_column(3)
    attend_column_over(3)
    attend_beside_over(2)
    kv_beside(3)
    opened.append(x_push(deep))
    for k in (1, 2, 3, 4):
        open_group(k)
    attend_beside(3)
    for k in (1, 2, 3):
        o_relay(k)
    attend_beside_over(3)
    for t in range(2):
        part_rows = slice(512 * t, 512 * t + 512)
        attn[t] = (
            mixed[part_rows, :] / jnp.sum(total[part_rows, :], axis=1, keepdims=True)
        ).astype(BF)


    def head_rows(head):
        return rows.at[:, aligned(head, HEAD)]

    def first_row(share):
        return jnp.clip(2 * share - 1, 0, 12)

    def needed(place):
        core, zhi, y = place
        return attn.at[core, pl.ds(pl.multiple_of(first_row(2 * y + zhi) * 32, 32), 128)]

    head = 2 * at.share + at.side
    first = first_row(at.share)
    role = at.core + at.side - 2 * at.core * at.side
    places = [(z, y) for z in (1, 0) for y in range(4)]
    arrivals = []
    for z, y in places:
        base = copies.reserve()
        copies.reserve()
        arrivals.append(base)
        for c in (0, 1):
            _, zhi, y_to = peer(0, z, y, 1)
            goal = (lax.rem(at.core + c, 2), zhi, y_to)
            device = {"x": px, **named(goal)}
            if (c, z, y) == (0, 0, 0):
                copies.hand(needed(goal), head_rows(head), device, native, base + role)
            else:
                copies.push(needed(goal), head_rows(head), device, base + role)
    def forward_group(k):
        block = ud_block(order[k], at.xb)
        copies.got(opened[k][0], block)
        forwarded.append(copies.push(block, block, {"x": at.xf}))

    def close_group(k):
        copies.got(opened[k][1], ud_block(order[k], at.xf))
        copies.got(forwarded[k], ud_block(order[k], at.xo))
        lump = ud_lump(order[k], at.core)
        lumps.append(copies.push(lump, lump, at.partner))

    shift = 2 * at.share - 1 - first
    for r in (1, 4):
        window[r] = jnp.zeros(window.shape[1:], F32)
    forward_group(0)
    forward_group(1)
    for k in range(4):
        o_last(k)
    for base, (z, y) in zip(arrivals, places):
        _, zhi, y_from = peer(0, z, y, -1)
        whose = 2 * (2 * y_from + zhi)
        copies.got(base, head_rows(whose + at.side))
        copies.got(base + 1, head_rows(whose + 1 - at.side))
    for k in range(4):
        for index, y in zip(o_over[k], (at.y, at.yb, at.yf, at.yo)):
            copies.got(index, wo_plane(y, 1 - at.core, k))
    for k in (5, 6, 7):
        open_group(k)
    forward_group(2)
    near_rows = pl.ds(pl.multiple_of(first * 32, 32), 128)

    def project(n, carry):
        columns = aligned(n, 768)
        acc = tok[at.core, near_rows, columns].astype(F32)
        for s in range(8):
            acc = acc + lax.dot_general(
                rows[:, 256 * s : 256 * s + 256],
                wo_here[s, pl.ds(4 * n, 4)].reshape(768, 256),
                (((1,), (1,)), ((), ())),
                preferred_element_type=F32,
            )
        residual[:, columns] = acc
        return carry

    lax.fori_loop(0, 4, project, 0)
    forward_group(3)
    forward_group(4)
    close_group(0)
    for r in range(4):
        row = residual[32 * r : 32 * r + 32, :]
        mean_square = jnp.mean(row * row, axis=1, keepdims=True)
        normed = row * lax.rsqrt(mean_square + 1e-06) * gain[...].astype(F32)
        window[1 + r - shift] = normed.astype(BF).astype(F32)
    close_group(1)
    line = lax.broadcasted_iota(jnp.int32, (32, 512), 0)

    def convolve(j):
        def tile(n, carry):
            columns = aligned(n, 512)
            sums = [jnp.zeros((32, 512), F32)] * 3
            for a in range(3):
                taps = conv[a, :, columns].astype(F32)
                values = window[1 + j + a, :, columns]
                for b in range(3):
                    sums[b] = sums[b] + values * taps[b : b + 1, :]
            before = jnp.where(line == 0, 0.0, pltpu.roll(sums[0], 1, 0))
            after = jnp.where(line == 31, 0.0, pltpu.roll(sums[2], 31, 0))
            gathered[aligned(2 * at.y + j, 32), columns] = (before + sums[1] + after).astype(BF)
            return carry

        lax.fori_loop(0, width // 512, tile, 0)

    def token_piece(y, h):
        return gathered.at[aligned(2 * y + h, 32)]

    ahead, behind = [], []
    for h in (0, 1):
        convolve(h)
        piece = token_piece(at.y, h)
        ahead.append(copies.push(piece, piece, {"y": at.yf}))
        behind.append(copies.push(piece, piece, {"y": at.yb}))
    forward_group(5)
    close_group(2)
    token_fwd = []
    for h in (0, 1):
        piece = token_piece(at.yb, h)
        copies.got(ahead[h], piece)
        token_fwd.append(copies.push(piece, piece, {"y": at.yf}))
    close_group(3)
    for k in (6, 7):
        forward_group(k)
    for k in (4, 5, 6, 7):
        close_group(k)
    for h in (0, 1):
        copies.got(behind[h], token_piece(at.yf, h))
        copies.got(token_fwd[h], token_piece(at.yo, h))
    for index, z in zip(lumps, order):
        copies.got(index, ud_lump(z, 1 - at.core))

    for n in range(3):
        columns = slice(256 * n, 256 * n + 256)
        value = jnp.dot(
            gathered[...],
            ud[0, :, :, :, columns].reshape(width, 256),
            preferred_element_type=F32,
        )
        hidden[:, columns] = jax.nn.gelu(value).astype(BF)

    chunk = width // 4

    def columns_of(q):
        return slice(chunk * q, chunk * q + chunk)

    def term(y, q):
        return terms.at[aligned(y, 64), pl.ds(chunk * q, chunk)]

    def strip(ref, q):
        return ref.at[:, pl.ds(chunk * q, chunk)]

    relays, directs, finals = [], [], []

    def pass_on(q):
        copies.got(relays[q], strip(relay, q))
        columns = columns_of(q)
        summed[:, columns] = (
            terms[aligned(at.yf, 64), columns].astype(F32) + relay[:, columns].astype(F32)
        ).astype(BF)
        finals.append(copies.push(strip(summed, q), strip(final, q), {"y": at.yf}))

    for q in range(4):
        terms[:, columns_of(q)] = lax.dot_general(
            hidden[...],
            ud[1, 4 * q : 4 * q + 4].reshape(chunk, chunk),
            (((1,), (1,)), ((), ())),
            preferred_element_type=F32,
        ).astype(BF)
        relays.append(copies.push(term(at.yo, q), strip(relay, q), {"y": at.yf}))
        directs.append(copies.push(term(at.yb, q), strip(direct, q), {"y": at.yb}))
        if q > 0:
            pass_on(q - 1)
    pass_on(3)
    own_rows = pl.ds(pl.multiple_of((1 + shift) * 32, 32), 64)
    for q in range(4):
        columns = columns_of(q)
        copies.got(directs[q], strip(direct, q))
        partial = (
            residual[own_rows, columns]
            + terms[aligned(at.y, 64), columns].astype(F32)
            + direct[:, columns].astype(F32)
        )
        copies.got(finals[q], strip(final, q))
        out[:, columns] = (partial + final[:, columns].astype(F32)).astype(BF)
    copies.sent()


def remote(collective_id, megabytes=32):
    return pltpu.CompilerParams(
        collective_id=collective_id, has_side_effects=True, vmem_limit_bytes=megabytes << 20
    )


def shape(*dims, dtype=BF):
    return jax.ShapeDtypeStruct(dims, dtype)


def shards(
    tokens, frame_time, qkv_weight, out_weight, norm_gain, conv_weight, up_weight, down_weight
):
    width = tokens.shape[3]
    result = pl.pallas_call(
        layer_kernel,
        out_shape=shape(64, width),
        in_specs=[SMEM] + [ANY] * 5 + [VMEM] * 2,
        out_specs=VMEM,
        scratch_shapes=[
            pltpu.VMEM((2, 512, width), BF),
            pltpu.VMEM((width, 3 * HEAD), BF),
            pltpu.VMEM((3, 1024, HEAD), BF),
            pltpu.VMEM((1024, HEAD), BF),
            pltpu.VMEM((16, 2, 1024, HEAD), BF),
            pltpu.VMEM((1024, HEAD), F32),
            pltpu.VMEM((1024, HEAD), F32),
            pltpu.VMEM((1024, HEAD), F32),
            pltpu.VMEM((2, 512, HEAD), BF),
            pltpu.VMEM((8, 16, 2, 96, 256), BF),
            pltpu.VMEM((128, 16 * HEAD), BF),
            pltpu.VMEM((128, width), F32),
            pltpu.VMEM((6, 32, width), F32),
            pltpu.VMEM((256, width), BF),
            pltpu.VMEM((2, 16, 2, 96, 768), BF),
            pltpu.VMEM((256, 768), BF),
            pltpu.VMEM((256, width), BF),
        ]
        + [pltpu.VMEM((64, width), BF)] * 4
        + scratch(288, 8),
        compiler_params=remote(1, 60),
    )(
        frame_time,
        tokens.reshape(64, width),
        qkv_weight,
        out_weight.T,
        up_weight,
        down_weight.T,
        norm_gain.reshape(1, width),
        conv_weight,
    )
    return result.reshape(1, 2, 32, width)


def solution(mesh):
    fine = Mesh(mesh.devices.reshape(4, 4, 2, 4, 2), AXES)
    frame, fsdp = ("zlo", "x", "core"), ("y", "zhi")
    placed = (
        P(frame, fsdp, None, None),
        P(),
        P(None, frame, fsdp),
        P(fsdp, frame),
        P(),
        P(),
        P(frame, fsdp),
        P(fsdp, frame),
    )
    return jax.shard_map(
        shards,
        mesh=fine,
        in_specs=placed,
        out_specs=P(frame, fsdp, None, None),
        check_vma=False,
    )
```
